128 devices in a mesh: row: 16 (over x, z), col: 8 (over y, core).
Axes of the slice: x: 4, y: 4, z: 4, core: 2. Of those that a mesh axis runs over, the one named last changes fastest.
Arguments:
- amplitudes: bfloat16 [64, 32, 512, 512], P('row', None, None, 'col'), may hold values from -6 to 6
- vvvv_ints: bfloat16 [512, 512, 8, 512], P('row', 'col'), may hold values from -0.015625 to 0.015625
- ovov_ints: bfloat16 [32, 8, 64, 512], P(None, None, 'row'), may hold values from -0.046875 to 0.046875
- occ_energy: float32 [64], replicated, may hold values from -2 to -0.5
- vir_energy: float32 [512], replicated, may hold values from 0.5 to 3
- occ_irrep: int32 [64], replicated, may hold values from 0 to 7, as said below
- vir_irrep: int32 [512], replicated, may hold values from 0 to 7, as said below
- i_orbitals: int32 [32], replicated, may hold values from 0 to 63, as said below
- j_orbitals: int32 [32], replicated, may hold values from 0 to 63, as said below
- a_orbitals: int32 [8], replicated, may hold values from 0 to 511, as said below
Outputs:
- update: float32 [32, 32, 8, 512], P('row', None, None, 'col')
The draws below stay inside these ranges and needn't reach their ends.
Inputs may be any that keep to these rules, and one draw needn't show every extreme that they name: `occ_irrep`: the orbitals form 8 contiguous runs of 8 each, one run for each label. `vir_irrep`: the orbitals form 8 contiguous runs of 64 each, one run for each label. `i_orbitals`: distinct occupied orbital numbers. `j_orbitals`: distinct occupied orbital numbers. `a_orbitals`: distinct virtual orbital numbers.
All inputs are finite; a program needn't handle non-finite values.
Results may differ from the reference program's by a relative error of at most 0.0003.
Values may be sent and summed in bfloat16 or wider, within the bound.
No kernel may reach another device: no remote copies, remote signals or barrier semaphores. Data moves between devices by JAX's collectives and lax.ppermute only.
A program may use at most 192 MiB of HBM per device.

```python
import jax
import jax.numpy as jnp
from jax import lax

NO = 64
NV = 512
OI = 32
OJ = 32
SA = 8


def pick_distinct(key, total, count):
    inner = jax.random.permutation(key, total - 2)[:count - 2].astype(jnp.int32) + 1
    ends = jnp.array([0, total - 1], dtype=jnp.int32)
    chosen = jnp.concatenate([ends, inner])
    order = jax.random.permutation(jax.random.fold_in(key, 5), count)
    return jnp.take(chosen, order).astype(jnp.int32)


def block_labels(key, total):
    labels = jax.random.permutation(key, 8).astype(jnp.int32)
    run_index = (jnp.arange(total, dtype=jnp.int32) // (total // 8)).astype(jnp.int32)
    return jnp.take(labels, run_index).astype(jnp.int32)


def draw_occ_irrep(key, part):
    key = jax.random.fold_in(key, 21)
    return block_labels(key, NO)


def draw_vir_irrep(key, part):
    key = jax.random.fold_in(key, 22)
    return block_labels(key, NV)


def draw_i_orbitals(key, part):
    key = jax.random.fold_in(key, 11)
    return pick_distinct(key, NO, OI)


def draw_j_orbitals(key, part):
    key = jax.random.fold_in(key, 12)
    return pick_distinct(key, NO, OJ)


def draw_a_orbitals(key, part):
    key = jax.random.fold_in(key, 13)
    return pick_distinct(key, NV, SA)


def with_spikes(values, key, source, target, parts, factor):
    def block_of(dim):
        return (jnp.arange(values.shape[dim]) // (values.shape[dim] // parts)).reshape((-1,) + (1,) * (values.ndim - 1 - dim))

    first = jax.random.permutation(key, parts)[block_of(target)]
    second = (block_of(target) + parts // 2) % parts
    return jnp.where((block_of(source) == first) | (block_of(source) == second), factor * values, values)


def block_scale(rng, dims, cuts, least, top_value):
    loudness = 1.0
    for position, blocks in cuts:
        draws = jax.random.uniform(jax.random.fold_in(jax.random.fold_in(rng, 6), position), (blocks,), jnp.float32, least / len(cuts), top_value / len(cuts))
        loudness = loudness * jnp.repeat(jnp.exp(draws), dims[position] // blocks).reshape((-1,) + (1,) * (len(dims) - 1 - position))
    return loudness


def gaussian(key, extent, width, reach, shards=(), kind=jnp.bfloat16):
    factor_of = block_scale(key, extent, shards, -0.22, 0.18) if shards else 1.0
    result = jax.random.normal(key, extent, jnp.float32) * width * factor_of
    return jnp.minimum(jnp.maximum(result, -reach), reach).astype(kind)


def bell_draw_with(own_key, extent, deviation, reach, split, heavy, held_as=jnp.bfloat16):
    drawn = deviation * jax.random.normal(own_key, extent, jnp.float32)
    if split:
        drawn = drawn * block_scale(own_key, extent, split, -0.22, 0.18)
    return jnp.clip(with_spikes(drawn, jax.random.fold_in(own_key, 3), *heavy), -reach, reach).astype(held_as)


def setup_inputs(seed: int = 0) -> dict:
    arg_keys = jax.random.split(jax.random.key(seed), 11)
    amplitudes = gaussian(arg_keys[0], (NO, OJ, NV, NV), 1.0, 6.0, ((0, 16), (3, 8)))
    vvvv_ints = bell_draw_with(arg_keys[1], (NV, NV, SA, NV), (NV * NV) ** -0.5, 0.015625, ((0, 16), (1, 8)), (1, 3, 8, 2.0))
    ovov_ints = bell_draw_with(arg_keys[2], (OI, SA, NO, NV), (NO * NV) ** -0.5, 0.046875, ((2, 16),), (2, 0, 16, 2.0))
    occ_energy = jnp.clip(jax.random.uniform(arg_keys[3], (NO,), jnp.float32, -2.0, -0.5), -2.0, -0.5)
    vir_energy = jnp.clip(jax.random.uniform(arg_keys[4], (NV,), jnp.float32, 0.5, 3.0), 0.5, 3.0)
    occ_irrep = draw_occ_irrep(jax.random.fold_in(arg_keys[10], 71), 0)
    vir_irrep = draw_vir_irrep(jax.random.fold_in(arg_keys[10], 71), 0)
    i_orbitals = draw_i_orbitals(jax.random.fold_in(arg_keys[10], 71), 0)
    j_orbitals = draw_j_orbitals(jax.random.fold_in(arg_keys[10], 71), 0)
    a_orbitals = draw_a_orbitals(jax.random.fold_in(arg_keys[10], 71), 0)
    return dict(amplitudes=amplitudes, vvvv_ints=vvvv_ints, ovov_ints=ovov_ints, occ_energy=occ_energy, vir_energy=vir_energy, occ_irrep=occ_irrep, vir_irrep=vir_irrep, i_orbitals=i_orbitals, j_orbitals=j_orbitals, a_orbitals=a_orbitals)


def reference(amplitudes, vvvv_ints, ovov_ints, occ_energy, vir_energy, occ_irrep, vir_irrep, i_orbitals, j_orbitals, a_orbitals):
    slab_rows = jnp.take(amplitudes, i_orbitals, axis=0).reshape(OI * OJ, NV, NV)
    block_width = NV // 16
    ints_flat = vvvv_ints.reshape(NV, NV * SA * NV)

    def add_block(block_step, running):
        first_c = (block_step * block_width).astype(jnp.int32)
        lower_part = lax.dynamic_slice_in_dim(slab_rows, first_c, block_width, 1).reshape(OI * OJ, block_width * NV)
        upper_part = lax.dynamic_slice_in_dim(ints_flat, first_c, block_width, 0).reshape(block_width * NV, SA * NV)
        return running + jnp.dot(lower_part, upper_part, preferred_element_type=jnp.float32)

    ladder = lax.fori_loop(0, 16, add_block, jnp.zeros((OI * OJ, SA * NV), jnp.float32))
    ladder = ladder.reshape(OI, OJ, SA, NV)
    reordered = amplitudes.transpose(0, 2, 1, 3).reshape(NO * NV, OJ * NV)
    cycle_term = jnp.dot(ovov_ints.reshape(OI * SA, NO * NV), reordered, preferred_element_type=jnp.float32)
    cycle_term = cycle_term.reshape(OI, SA, OJ, NV).transpose(0, 2, 1, 3)
    combined = ladder + cycle_term
    occ_i_energy = jnp.take(occ_energy, i_orbitals)
    occ_j_energy = jnp.take(occ_energy, j_orbitals)
    vir_a_energy = jnp.take(vir_energy, a_orbitals)
    denominator = occ_i_energy[:, None, None, None] + occ_j_energy[None, :, None, None] - vir_a_energy[None, None, :, None] - vir_energy[None, None, None, :]
    sym_i = jnp.take(occ_irrep, i_orbitals)
    sym_j = jnp.take(occ_irrep, j_orbitals)
    sym_a = jnp.take(vir_irrep, a_orbitals)
    product_irrep = jnp.bitwise_xor(jnp.bitwise_xor(sym_i[:, None, None, None], sym_j[None, :, None, None]), jnp.bitwise_xor(sym_a[None, None, :, None], vir_irrep[None, None, None, :]))
    allowed = product_irrep == 0
    return jnp.where(allowed, combined / denominator, jnp.zeros_like(combined)).astype(jnp.float32)
```

```python
import functools

import jax
import jax.numpy as jnp
import numpy as np
from jax import lax
from jax.experimental import pallas as pl
from jax.experimental.pallas import tpu as pltpu
from jax.sharding import PartitionSpec as P

F32 = jnp.float32
BF16 = jnp.bfloat16
VMEM = 48 * 1024 * 1024

NO, NV, OI, OJ, SA = 64, 512, 32, 32, 8
ROWS, COLS, RUN = 16, 8, 64
PIECES = 4
DP = 64 // PIECES
QP = DP // 4
KP = DP * 32


def params(n=1):
    return pltpu.CompilerParams(
        dimension_semantics=("arbitrary",) * n, vmem_limit_bytes=VMEM
    )


def cost(flops, nbytes):
    return pl.CostEstimate(flops=flops, bytes_accessed=nbytes, transcendentals=0)


def one_hot_swap(m, n):
    out = np.zeros((m * n, m * n), np.float32)
    for a in range(m):
        for b in range(n):
            out[b * m + a, a * n + b] = 1
    return out.astype(jnp.bfloat16)


def lane_swap():
    out = np.zeros((4, 4, 32, 4, 4, 32), np.float32)
    for e in range(4):
        for z in range(4):
            for c in range(32):
                out[e, z, c, z, e, c] = 1
    return out.reshape(512, 512).astype(jnp.bfloat16)


def pack_kernel(x_ref, swap_ref, lanes_ref, out_ref, mid_ref):
    for jh in range(2):
        for dh in range(DP // 16):
            x = x_ref[0, 16 * jh : 16 * jh + 16, 16 * dh : 16 * dh + 16, :].reshape(256, NV)
            y = jnp.dot(swap_ref[...], x, preferred_element_type=F32).astype(BF16)
            mid_ref[16 * dh : 16 * dh + 16, 16 * jh : 16 * jh + 16, :] = y.reshape(16, 16, NV)
    for q in range(QP):
        for x in range(4):
            z = jnp.concatenate(
                [mid_ref[4 * q + e, :, 128 * x : 128 * x + 128] for e in range(4)], axis=1
            )
            w = jnp.dot(z, lanes_ref[...], preferred_element_type=F32).astype(BF16)
            for zz in range(4):
                out_ref[4 * x + zz, q, 0, :, :] = w[:, 128 * zz : 128 * zz + 128]


def pack(amp_t, piece):
    return pl.pallas_call(
        pack_kernel,
        grid=(4,),
        in_specs=[
            pl.BlockSpec((1, OJ, DP, NV), lambda k: (k, 0, piece, 0)),
            pl.BlockSpec((256, 256), lambda k: (0, 0)),
            pl.BlockSpec((512, 512), lambda k: (0, 0)),
        ],
        out_specs=pl.BlockSpec((ROWS, QP, 1, OJ, 128), lambda k: (0, 0, k, 0, 0)),
        out_shape=jax.ShapeDtypeStruct((ROWS, QP, 4, OJ, 128), BF16),
        scratch_shapes=[pltpu.VMEM((DP, OJ, NV), BF16)],
        compiler_params=params(),
        cost_estimate=cost(6_400_000_000 // PIECES, 2 * 8 * 2**20 // PIECES),
        name="pack",
    )(amp_t, one_hot_swap(16, 16), lane_swap())


def ints_kernel(gtab_ref, v_ref, swap_ref, out_ref):
    halves = []
    for ch in range(2):
        x = v_ref[16 * ch : 16 * ch + 16, :, :].reshape(256, NV)
        y = jnp.dot(swap_ref[...], x, preferred_element_type=F32)
        halves.append(y.reshape(2, SA, 16, NV))
    for a in range(SA):
        off = 64 * (a % 2)
        for t in range(4):
            tile = jnp.concatenate(
                [halves[ch][d, a, :, 128 * t : 128 * t + 128] for d in range(2) for ch in range(2)],
                axis=0,
            )
            turned = pltpu.roll(tile, 64, 1)
            for e in range(2):
                src = tile if e == a % 2 else turned
                g = gtab_ref[a, 2 * t + e]
                out_ref[0, g, :, 64 * a : 64 * a + 64] = src[:, off : off + 64].astype(BF16)


def arrange_ints(gtab, ints):
    steps = 32 // PIECES
    return pl.pallas_call(
        ints_kernel,
        grid_spec=pltpu.PrefetchScalarGridSpec(
            num_scalar_prefetch=1,
            grid=(32,),
            in_specs=[
                pl.BlockSpec((32, 16, NV), lambda s, *_: (0, s, 0)),
                pl.BlockSpec((256, 256), lambda s, *_: (0, 0)),
            ],
            out_specs=pl.BlockSpec(
                (1, 8, 64, NV), lambda s, *_: (s // steps, 0, s % steps, 0)
            ),
        ),
        out_shape=jax.ShapeDtypeStruct((PIECES, 8, KP, SA * RUN), BF16),
        compiler_params=params(),
        cost_estimate=cost(4_300_000_000, 32 * 2**20),
        name="arrange_ints",
    )(gtab, ints, one_hot_swap(16, 16))


def two_terms(x):
    hi = x.astype(BF16)
    return hi, (x - hi.astype(F32)).astype(BF16)


def gather_rows(iorb_ref, r_ref, pick_ref, rows_ref):
    for blk in range(8):
        slabs = []
        for i in range(4):
            k = iorb_ref[4 * blk + i]
            slabs.append(
                jnp.concatenate([r_ref[k // 4, q, k % 4, :, :] for q in range(QP)], axis=1)
            )
        x = jnp.concatenate(slabs, axis=0)
        y = jnp.dot(pick_ref[blk], x, preferred_element_type=F32).astype(BF16)
        rows_ref[:, 32 * blk : 32 * blk + 32, :] = y.reshape(8, 32, KP)


def ladder_kernel(first, iorb_ref, r_ref, pick_ref, ints_ref, *rest):
    if first:
        out_ref, rows_ref = rest
    else:
        acc_ref, out_ref, rows_ref = rest
    g = pl.program_id(0)

    @pl.when(g == 0)
    def _():
        gather_rows(iorb_ref, r_ref, pick_ref, rows_ref)

    got = jnp.dot(rows_ref[g], ints_ref[0, 0], preferred_element_type=F32)
    out_ref[0] = got if first else got + acc_ref[0]


def last_kernel(iorb_ref, core_ref, r_ref, pick_ref, ints_ref, acc_ref, drop_ref, cycle_ref,
                keep_ref, send_ref, rows_ref, sum_ref):
    g = pl.program_id(0)

    @pl.when(g == 0)
    def _():
        gather_rows(iorb_ref, r_ref, pick_ref, rows_ref)

    sum_ref[g] = acc_ref[0] + jnp.dot(rows_ref[g], ints_ref[0, 0], preferred_element_type=F32)

    @pl.when(g == 7)
    def _():
        core = core_ref[0]
        for blk in range(8):
            x = sum_ref[:, 32 * blk : 32 * blk + 32, :].reshape(256, SA * RUN)
            hi, lo = two_terms(x)
            y = jnp.dot(drop_ref[blk], hi, preferred_element_type=F32)
            y = y + jnp.dot(drop_ref[blk], lo, preferred_element_type=F32)
            for i in range(4):
                p = 4 * blk + i
                got = y[32 * i : 32 * i + 32, :] + cycle_ref[p]

                @pl.when(core == p % 2)
                def _():
                    keep_ref[p // 2] = got

                @pl.when(core != p % 2)
                def _():
                    send_ref[p // 2] = got


def ladder(piece, iorb, core, arrived, pick, ints, acc, drop, cyc):
    first, last = piece == 0, piece == PIECES - 1
    n_scalar = 2 if last else 1
    whole = lambda *dims: pl.BlockSpec(dims, lambda g, *_: (0,) * len(dims))
    acc_spec = pl.BlockSpec((1, 256, 512), lambda g, *_: (g, 0, 0))
    in_specs = [
        whole(ROWS, QP, 4, OJ, 128),
        whole(8, 256, 128),
        pl.BlockSpec((1, 1, KP, 512), lambda g, *_: (piece, g, 0, 0)),
    ]
    args = [arrived, pick, ints]
    if not first:
        in_specs.append(acc_spec)
        args.append(acc)
    scratch = [pltpu.VMEM((8, 256, KP), BF16)]
    if last:
        in_specs += [whole(8, 128, 256), whole(OI, OJ, 512)]
        args += [drop, cyc]
        out_specs = [whole(16, OJ, 512)] * 2
        out_shape = [jax.ShapeDtypeStruct((16, OJ, 512), F32)] * 2
        scratch.append(pltpu.VMEM((8, 256, 512), F32))
        body, scalars = last_kernel, [iorb, core]
    else:
        out_specs = acc_spec
        out_shape = jax.ShapeDtypeStruct((8, 256, 512), F32)
        body, scalars = functools.partial(ladder_kernel, first), [iorb]
    return pl.pallas_call(
        body,
        grid_spec=pltpu.PrefetchScalarGridSpec(
            num_scalar_prefetch=n_scalar,
            grid=(8,),
            in_specs=in_specs,
            out_specs=out_specs,
            scratch_shapes=scratch,
        ),
        out_shape=out_shape,
        compiler_params=params(),
        cost_estimate=cost(5_400_000_000 // PIECES, 14 * 2**20),
        name="ladder",
    )(*scalars, *args)


def by_run_kernel(ltab_ref, x_ref, spread_ref, out_ref):
    hi, lo = two_terms(jnp.sum(x_ref[...], axis=0))
    y = jnp.dot(spread_ref[...], hi, preferred_element_type=F32)
    y = y + jnp.dot(spread_ref[...], lo, preferred_element_type=F32)
    for a in range(SA):
        for t in range(8):
            out_ref[ltab_ref[a, t], :, 64 * a : 64 * a + 64] = y[8 * t : 8 * t + 8, 64 * a : 64 * a + 64]


def by_run(ltab, x, spread):
    return pl.pallas_call(
        by_run_kernel,
        grid_spec=pltpu.PrefetchScalarGridSpec(
            num_scalar_prefetch=1,
            grid=(1,),
            in_specs=[
                pl.BlockSpec((ROWS, OJ, 512), lambda s, *_: (0, 0, 0)),
                pl.BlockSpec((64, OJ), lambda s, *_: (0, 0)),
            ],
            out_specs=pl.BlockSpec((8, 8, 512), lambda s, *_: (0, 0, 0)),
        ),
        out_shape=jax.ShapeDtypeStruct((8, 8, 512), F32),
        compiler_params=params(),
        name="by_run",
    )(ltab, x, spread)


def finish_kernel(slot_ref, irr_ref, energy_ref, x_ref, va_ref, vb_ref, sa_ref, sb_ref, out_ref, tile_ref):
    for h in range(2):
        v = x_ref[h]
        for y in range(1, 4):
            v = v + x_ref[2 * y + h]
        for a in range(SA):
            tile_ref[h, :, a, :] = v[:, 64 * a : 64 * a + 64]
    sym_ab = jnp.bitwise_xor(sa_ref[...], sb_ref[...])
    for h in range(2):
        for j in range(OJ):
            got = tile_ref[h, slot_ref[j]]
            den = energy_ref[h, j] - va_ref[...] - vb_ref[...]
            ok = jnp.bitwise_xor(sym_ab, irr_ref[h, j]) == 0
            out_ref[h, j] = jnp.where(ok, got / den, jnp.zeros_like(got))


def finish(slot, irr, energy, x, va, vb, sa, sb):
    full = lambda *dims: pl.BlockSpec(dims, lambda s, *_: (0,) * len(dims))
    return pl.pallas_call(
        finish_kernel,
        grid_spec=pltpu.PrefetchScalarGridSpec(
            num_scalar_prefetch=3,
            grid=(1,),
            in_specs=[full(8, 8, 512), full(8, 64), full(8, 64), full(8, 64), full(8, 64)],
            out_specs=full(2, OJ, SA, RUN),
            scratch_shapes=[pltpu.VMEM((2, 8, SA, RUN), F32)],
        ),
        out_shape=jax.ShapeDtypeStruct((2, OJ, SA, RUN), F32),
        compiler_params=params(),
        name="finish",
    )(slot, irr, energy, x, va, vb, sa, sb)


def shards(
    amplitudes,
    vvvv_ints,
    ovov_ints,
    occ_energy,
    vir_energy,
    occ_irrep,
    vir_irrep,
    i_orbitals,
    j_orbitals,
    a_orbitals,
):
    row = lax.axis_index("row")
    col = lax.axis_index("col")
    core = lax.rem(col, 2)
    labels = jnp.arange(8, dtype=jnp.int32)

    amp_t = amplitudes.transpose(0, 1, 3, 2)
    arrived = []
    for piece in range(PIECES):
        sent = pack(amp_t, piece)
        arrived.append(lax.all_to_all(sent, "row", split_axis=0, concat_axis=0, tiled=True))

    sym_i = jnp.take(occ_irrep, i_orbitals)
    sym_j = jnp.take(occ_irrep, j_orbitals)
    sym_a = jnp.take(vir_irrep, a_orbitals)
    run_label = vir_irrep.reshape(8, RUN)[:, 0]
    slot = j_orbitals % 8
    gtab = jnp.bitwise_xor(sym_a[:, None], run_label[None, :])
    g_ij = jnp.bitwise_xor(sym_i[:, None], sym_j[None, :])
    hit = (g_ij[:, :, None, None] == labels[:, None]) & (slot[:, None, None] == labels)
    hit = hit.reshape(8, 4, OJ, 8, 8)
    same = (jnp.arange(4)[:, None] == jnp.arange(4)).reshape(1, 4, 1, 1, 4, 1)
    drop = (hit[:, :, :, :, None, :] & same).reshape(8, 128, 256).astype(BF16)
    pick = drop.transpose(0, 2, 1)

    ints = arrange_ints(gtab, vvvv_ints.reshape(32, 512, NV))

    cyc = jnp.einsum("iakc,kjcb->ijab", ovov_ints, amplitudes, preferred_element_type=F32)
    mine_label = lax.dynamic_index_in_dim(run_label, col, keepdims=False)
    wanted = jnp.bitwise_xor(g_ij[:, :, None], sym_a) == mine_label
    cyc = jnp.where(wanted[..., None], cyc, 0.0).reshape(OI, OJ, SA * RUN)

    acc = None
    core1 = core.reshape(1)
    for piece in range(PIECES):
        acc = ladder(piece, i_orbitals, core1, arrived[piece], pick, ints, acc, drop, cyc)
    keep, send = acc

    got = lax.ppermute(send, "col", [(q, q ^ 1) for q in range(COLS)])
    both = lax.all_to_all(keep + got, "row", split_axis=0, concat_axis=0, tiled=True)

    mine_i = lax.dynamic_slice_in_dim(i_orbitals, 2 * row, 2)
    sym_mine = jnp.take(occ_irrep, mine_i)
    label_at = jnp.bitwise_xor(
        jnp.bitwise_xor(lax.dynamic_index_in_dim(sym_mine, core, keepdims=False), sym_a)[:, None],
        labels[None, :],
    )
    ltab = jnp.sum(jnp.where(label_at[..., None] == run_label, labels, 0), axis=-1).astype(jnp.int32)
    spread = (
        (sym_j[None, None, :] == labels[:, None, None]) & (slot[None, None, :] == labels[None, :, None])
    ).reshape(64, OJ).astype(BF16)
    parts = lax.all_to_all(by_run(ltab, both, spread), "col", split_axis=0, concat_axis=0, tiled=True)

    energy = jnp.take(occ_energy, mine_i)[:, None] + jnp.take(occ_energy, j_orbitals)[None, :]
    irr = jnp.bitwise_xor(sym_mine[:, None], sym_j[None, :])
    wide = lambda x: jnp.broadcast_to(x, (SA, RUN))
    va = wide(jnp.take(vir_energy, a_orbitals)[:, None])
    vb = wide(lax.dynamic_slice_in_dim(vir_energy, col * RUN, RUN)[None, :])
    sa = wide(sym_a[:, None])
    sb = wide(lax.dynamic_slice_in_dim(vir_irrep, col * RUN, RUN)[None, :])
    return finish(slot, irr, energy, parts, va, vb, sa, sb)


def solution(mesh):
    return jax.shard_map(
        shards,
        mesh=mesh,
        in_specs=(
            P("row", None, None, "col"),
            P("row", "col", None, None),
            P(None, None, "row", None),
            P(),
            P(),
            P(),
            P(),
            P(),
            P(),
            P(),
        ),
        out_specs=P("row", None, None, "col"),
        check_vma=False,
    )
```

```python
import functools

import jax
import jax.numpy as jnp
import numpy as np
from jax import lax
from jax.experimental import pallas as pl
from jax.experimental.pallas import tpu as pltpu
from jax.sharding import PartitionSpec as P

F32 = jnp.float32
BF16 = jnp.bfloat16
VMEM = 22 * 1024 * 1024

NO, NV, OI, OJ, SA = 64, 512, 32, 32, 8
ROWS, COLS, RUN = 16, 8, 64
PIECES = 2
DP = 64 // PIECES
QP = DP // 4
KP = DP * 32


def params(n=1):
    return pltpu.CompilerParams(
        dimension_semantics=("arbitrary",) * n, vmem_limit_bytes=VMEM
    )


def in_hbm(x):
    return pltpu.with_memory_space_constraint(x, pltpu.HBM)


def in_vmem(x):
    return pltpu.with_memory_space_constraint(x, pltpu.VMEM)


def cost(flops, nbytes):
    return pl.CostEstimate(flops=flops, bytes_accessed=nbytes, transcendentals=0)


def lane_swap():
    out = np.zeros((4, 4, 32, 4, 4, 32), np.float32)
    for e in range(4):
        for z in range(4):
            for c in range(32):
                out[e, z, c, z, e, c] = 1
    return out.reshape(512, 512).astype(jnp.bfloat16)


def pack_kernel(x_ref, lanes_ref, out_ref, mid_ref):
    for jh in range(2):
        rows = slice(16 * jh, 16 * jh + 16)
        for dh in range(DP // 16):
            y = jnp.swapaxes(x_ref[0, rows, 16 * dh : 16 * dh + 16, :], 0, 1)
            for q in range(4):
                for e in range(4):
                    for x in range(4):
                        mid_ref[x, 4 * dh + q, rows, 128 * e : 128 * e + 128] = y[
                            4 * q + e, :, 128 * x : 128 * x + 128
                        ]
    for x in range(4):
        w = jnp.dot(mid_ref[x].reshape(QP * OJ, 512), lanes_ref[...], preferred_element_type=F32)
        w = w.astype(BF16)
        for z in range(4):
            out_ref[4 * x + z, 0] = w[:, 128 * z : 128 * z + 128].reshape(QP, OJ, 128)


def pack(amp_t, piece):
    return pl.pallas_call(
        pack_kernel,
        grid=(4,),
        in_specs=[
            pl.BlockSpec((1, OJ, DP, NV), lambda k: (k, 0, piece, 0)),
            pl.BlockSpec((512, 512), lambda k: (0, 0)),
        ],
        out_specs=pl.BlockSpec((ROWS, 1, QP, OJ, 128), lambda k: (0, k, 0, 0, 0)),
        out_shape=pltpu.HBM((ROWS, 4, QP, OJ, 128), BF16),
        scratch_shapes=[pltpu.VMEM((4, QP, OJ, 512), BF16)],
        compiler_params=params(),
        cost_estimate=cost(8_000_000_000 // PIECES, 2 * 8 * 2**20 // PIECES),
        name="pack",
    )(in_hbm(amp_t), in_hbm(jnp.asarray(lane_swap())))


IN_STEP = 8


def ints_kernel(gtab_ref, v_ref, out_ref):
    for dd in range(IN_STEP // 2):
        for ch in range(2):
            x = v_ref[16 * ch : 16 * ch + 16, 16 * dd : 16 * dd + 16, :]
            y = jnp.swapaxes(x, 0, 1)
            for d in range(2):
                row = 64 * dd + 32 * d + 16 * ch
                for a in range(SA):
                    off = 64 * (a % 2)
                    for t in range(4):
                        tile = y[8 * d + a, :, 128 * t : 128 * t + 128]
                        for e in range(2):
                            part = tile[:, 64 * e : 64 * e + 64]
                            out_ref[gtab_ref[a, 2 * t + e], row : row + 16, 64 * a : 64 * a + 64] = part


def arrange_ints(piece, gtab, ints):
    steps = DP // IN_STEP
    return pl.pallas_call(
        ints_kernel,
        grid_spec=pltpu.PrefetchScalarGridSpec(
            num_scalar_prefetch=1,
            grid=(steps,),
            in_specs=[pl.BlockSpec((32, 8 * IN_STEP, NV), lambda s, *_: (0, piece * steps + s, 0))],
            out_specs=pl.BlockSpec((8, 32 * IN_STEP, NV), lambda s, *_: (0, s, 0)),
        ),
        out_shape=jax.ShapeDtypeStruct((8, KP, SA * RUN), BF16),
        compiler_params=params(),
        cost_estimate=cost(4_300_000_000, 32 * 2**20 // PIECES),
        name="arrange_ints",
    )(gtab, in_hbm(ints))


def two_terms(x):
    hi = x.astype(BF16)
    return hi, (x - hi.astype(F32)).astype(BF16)


def gather_rows(iorb_ref, r_ref, pick_ref, rows_ref, slab_ref, sems):
    def slab(p):
        k = iorb_ref[p]
        return pltpu.make_async_copy(r_ref.at[k // 4, k % 4], slab_ref.at[p], sems.at[p])

    def start(p, carry):
        slab(p).start()
        return carry

    def block(blk, carry):
        slabs = []
        for i in range(4):
            slab(4 * blk + i).wait()
        for i in range(4):
            slabs.append(
                jnp.concatenate([slab_ref[4 * blk + i, q] for q in range(QP)], axis=1)
            )
        x = jnp.concatenate(slabs, axis=0)
        y = jnp.dot(pick_ref[blk], x, preferred_element_type=F32).astype(BF16)
        rows_ref[:, pl.ds(pl.multiple_of(32 * blk, 32), 32), :] = y.reshape(8, 32, KP)
        return carry

    lax.fori_loop(0, OI, start, 0)
    lax.fori_loop(0, 8, block, 0)


GATHER_SCRATCH = [
    pltpu.VMEM((8, 256, KP), BF16),
    pltpu.VMEM((OI, QP, OJ, 128), BF16),
    pltpu.SemaphoreType.DMA((OI,)),
]


def ladder_kernel(first, iorb_ref, r_ref, pick_ref, ints_ref, *rest):
    if first:
        out_ref, rows_ref, slab_ref, sems = rest
    else:
        acc_ref, out_ref, rows_ref, slab_ref, sems = rest
    g = pl.program_id(0)

    @pl.when(g == 0)
    def _():
        gather_rows(iorb_ref, r_ref, pick_ref, rows_ref, slab_ref, sems)

    got = jnp.dot(rows_ref[g], ints_ref[0], preferred_element_type=F32)
    out_ref[0] = got if first else got + acc_ref[0]


def last_kernel(iorb_ref, core_ref, r_ref, pick_ref, ints_ref, acc_ref, drop_ref, cycle_ref,
                keep_ref, send_ref, rows_ref, slab_ref, sems, sum_ref):
    core = core_ref[0]
    gather_rows(iorb_ref, r_ref, pick_ref, rows_ref, slab_ref, sems)

    def group(g, carry):
        sum_ref[g] = acc_ref[g] + jnp.dot(rows_ref[g], ints_ref[g], preferred_element_type=F32)
        return carry

    lax.fori_loop(0, 8, group, 0)

    def block(blk, carry):
        x = sum_ref[:, pl.ds(pl.multiple_of(32 * blk, 32), 32), :].reshape(256, SA * RUN)
        hi, lo = two_terms(x)
        y = jnp.dot(drop_ref[blk], hi, preferred_element_type=F32)
        y = y + jnp.dot(drop_ref[blk], lo, preferred_element_type=F32)
        for i in range(4):
            got = y[32 * i : 32 * i + 32, :] + cycle_ref[4 * blk + i]

            @pl.when(core == i % 2)
            def _():
                keep_ref[2 * blk + i // 2] = got

            @pl.when(core != i % 2)
            def _():
                send_ref[2 * blk + i // 2] = got

        return carry

    lax.fori_loop(0, 8, block, 0)


def ladder(first, iorb, arrived, pick, ints, acc):
    whole = lambda *dims: pl.BlockSpec(dims, lambda g, *_: (0,) * len(dims))
    acc_spec = pl.BlockSpec((1, 256, 512), lambda g, *_: (g, 0, 0))
    in_specs = [
        pl.BlockSpec(memory_space=pltpu.HBM),
        whole(8, 256, 128),
        pl.BlockSpec((1, KP, 512), lambda g, *_: (g, 0, 0)),
    ]
    args = [in_hbm(arrived), pick, ints]
    if not first:
        in_specs.append(acc_spec)
        args.append(acc)
    return pl.pallas_call(
        functools.partial(ladder_kernel, first),
        grid_spec=pltpu.PrefetchScalarGridSpec(
            num_scalar_prefetch=1,
            grid=(8,),
            in_specs=in_specs,
            out_specs=acc_spec,
            scratch_shapes=GATHER_SCRATCH,
        ),
        out_shape=jax.ShapeDtypeStruct((8, 256, 512), F32),
        compiler_params=params(),
        cost_estimate=cost(5_400_000_000 // PIECES, 14 * 2**20),
        name="ladder",
    )(iorb, *args)


def last_ladder(iorb, core, arrived, *args):
    smem = pl.BlockSpec(memory_space=pltpu.SMEM)
    vmem = pl.BlockSpec(memory_space=pltpu.VMEM)
    return pl.pallas_call(
        last_kernel,
        in_specs=[smem, smem, pl.BlockSpec(memory_space=pltpu.HBM)] + [vmem] * len(args),
        out_specs=[vmem] * 2,
        out_shape=[jax.ShapeDtypeStruct((16, OJ, 512), F32)] * 2,
        scratch_shapes=GATHER_SCRATCH + [pltpu.VMEM((8, 256, 512), F32)],
        compiler_params=pltpu.CompilerParams(vmem_limit_bytes=VMEM),
        cost_estimate=cost(5_400_000_000 // PIECES, 14 * 2**20),
        name="last_ladder",
    )(iorb, core, in_hbm(arrived), *[in_vmem(x) for x in args])


def by_run_kernel(ltab_ref, x_ref, spread_ref, out_ref):
    hi, lo = two_terms(jnp.sum(x_ref[...], axis=0))
    y = jnp.dot(spread_ref[...], hi, preferred_element_type=F32)
    y = y + jnp.dot(spread_ref[...], lo, preferred_element_type=F32)
    for a in range(SA):
        for t in range(8):
            out_ref[ltab_ref[a, t], :, 64 * a : 64 * a + 64] = y[8 * t : 8 * t + 8, 64 * a : 64 * a + 64]


def by_run(ltab, x, spread):
    return pl.pallas_call(
        by_run_kernel,
        grid_spec=pltpu.PrefetchScalarGridSpec(
            num_scalar_prefetch=1,
            grid=(1,),
            in_specs=[
                pl.BlockSpec((ROWS, OJ, 512), lambda s, *_: (0, 0, 0)),
                pl.BlockSpec((64, OJ), lambda s, *_: (0, 0)),
            ],
            out_specs=pl.BlockSpec((8, 8, 512), lambda s, *_: (0, 0, 0)),
        ),
        out_shape=jax.ShapeDtypeStruct((8, 8, 512), F32),
        compiler_params=params(),
        name="by_run",
    )(ltab, x, spread)


def finish_kernel(slot_ref, irr_ref, energy_ref, x_ref, va_ref, vb_ref, sa_ref, sb_ref, out_ref, tile_ref):
    for h in range(2):
        v = x_ref[h]
        for y in range(1, 4):
            v = v + x_ref[2 * y + h]
        for a in range(SA):
            tile_ref[h, :, a, :] = v[:, 64 * a : 64 * a + 64]
    sym_ab = jnp.bitwise_xor(sa_ref[...], sb_ref[...])
    for h in range(2):
        for j in range(OJ):
            got = tile_ref[h, slot_ref[j]]
            den = energy_ref[h, j] - va_ref[...] - vb_ref[...]
            ok = jnp.bitwise_xor(sym_ab, irr_ref[h, j]) == 0
            out_ref[h, j] = jnp.where(ok, got / den, jnp.zeros_like(got))


def finish(slot, irr, energy, x, va, vb, sa, sb):
    full = lambda *dims: pl.BlockSpec(dims, lambda s, *_: (0,) * len(dims))
    return pl.pallas_call(
        finish_kernel,
        grid_spec=pltpu.PrefetchScalarGridSpec(
            num_scalar_prefetch=3,
            grid=(1,),
            in_specs=[full(8, 8, 512), full(8, 64), full(8, 64), full(8, 64), full(8, 64)],
            out_specs=full(2, OJ, SA, RUN),
            scratch_shapes=[pltpu.VMEM((2, 8, SA, RUN), F32)],
        ),
        out_shape=jax.ShapeDtypeStruct((2, OJ, SA, RUN), F32),
        compiler_params=params(),
        name="finish",
    )(slot, irr, energy, x, va, vb, sa, sb)


def shards(
    amplitudes,
    vvvv_ints,
    ovov_ints,
    occ_energy,
    vir_energy,
    occ_irrep,
    vir_irrep,
    i_orbitals,
    j_orbitals,
    a_orbitals,
):
    row = lax.axis_index("row")
    col = lax.axis_index("col")
    core = lax.rem(col, 2)
    labels = jnp.arange(8, dtype=jnp.int32)

    amp_t = amplitudes.transpose(0, 1, 3, 2)
    arrived = []
    for piece in range(PIECES):
        sent = pack(amp_t, piece)
        arrived.append(lax.all_to_all(sent, "row", split_axis=0, concat_axis=0, tiled=True))

    sym_i = jnp.take(occ_irrep, i_orbitals)
    sym_j = jnp.take(occ_irrep, j_orbitals)
    sym_a = jnp.take(vir_irrep, a_orbitals)
    run_label = vir_irrep.reshape(8, RUN)[:, 0]
    slot = j_orbitals % 8
    gtab = jnp.bitwise_xor(sym_a[:, None], run_label[None, :])
    g_ij = jnp.bitwise_xor(sym_i[:, None], sym_j[None, :])
    hit = (g_ij[:, :, None, None] == labels[:, None]) & (slot[:, None, None] == labels)
    hit = hit.reshape(8, 4, OJ, 8, 8)
    same = (jnp.arange(4)[:, None] == jnp.arange(4)).reshape(1, 4, 1, 1, 4, 1)
    drop = (hit[:, :, :, :, None, :] & same).reshape(8, 128, 256).astype(BF16)
    pick = drop.transpose(0, 2, 1)

    ints = [arrange_ints(piece, gtab, vvvv_ints.reshape(32, 512, NV)) for piece in range(PIECES)]

    cyc = jnp.einsum("iakc,kjcb->ijab", ovov_ints, amplitudes, preferred_element_type=F32)
    mine_label = lax.dynamic_index_in_dim(run_label, col, keepdims=False)
    wanted = jnp.bitwise_xor(g_ij[:, :, None], sym_a) == mine_label
    cyc = jnp.where(wanted[..., None], cyc, 0.0).reshape(OI, OJ, SA * RUN)

    acc = None
    for piece in range(PIECES - 1):
        acc = ladder(piece == 0, i_orbitals, arrived[piece], pick, ints[piece], acc)
    keep, send = last_ladder(i_orbitals, core.reshape(1), arrived[-1], pick, ints[-1], acc, drop, cyc)

    got = lax.ppermute(send, "col", [(q, q ^ 1) for q in range(COLS)])
    both = lax.all_to_all(keep + got, "row", split_axis=0, concat_axis=0, tiled=True)

    mine_i = lax.dynamic_slice_in_dim(i_orbitals, 2 * row, 2)
    sym_mine = jnp.take(occ_irrep, mine_i)
    label_at = jnp.bitwise_xor(
        jnp.bitwise_xor(lax.dynamic_index_in_dim(sym_mine, core, keepdims=False), sym_a)[:, None],
        labels[None, :],
    )
    ltab = jnp.sum(jnp.where(label_at[..., None] == run_label, labels, 0), axis=-1).astype(jnp.int32)
    spread = (
        (sym_j[None, None, :] == labels[:, None, None]) & (slot[None, None, :] == labels[None, :, None])
    ).reshape(64, OJ).astype(BF16)
    parts = lax.all_to_all(by_run(ltab, both, spread), "col", split_axis=0, concat_axis=0, tiled=True)

    energy = jnp.take(occ_energy, mine_i)[:, None] + jnp.take(occ_energy, j_orbitals)[None, :]
    irr = jnp.bitwise_xor(sym_mine[:, None], sym_j[None, :])
    wide = lambda x: jnp.broadcast_to(x, (SA, RUN))
    va = wide(jnp.take(vir_energy, a_orbitals)[:, None])
    vb = wide(lax.dynamic_slice_in_dim(vir_energy, col * RUN, RUN)[None, :])
    sa = wide(sym_a[:, None])
    sb = wide(lax.dynamic_slice_in_dim(vir_irrep, col * RUN, RUN)[None, :])
    return finish(slot, irr, energy, parts, va, vb, sa, sb)


def solution(mesh):
    return jax.shard_map(
        shards,
        mesh=mesh,
        in_specs=(
            P("row", None, None, "col"),
            P("row", "col", None, None),
            P(None, None, "row", None),
            P(),
            P(),
            P(),
            P(),
            P(),
            P(),
            P(),
        ),
        out_specs=P("row", None, None, "col"),
        check_vma=False,
    )
```

```python
import functools

import jax
import jax.numpy as jnp
import numpy as np
from jax import lax
from jax.experimental import pallas as pl
from jax.experimental.pallas import tpu as pltpu
from jax.sharding import PartitionSpec as P

F32 = jnp.float32
BF16 = jnp.bfloat16
VMEM = 50 * 1024 * 1024

NO, NV, OI, OJ, SA = 64, 512, 32, 32, 8
ROWS, COLS, RUN = 16, 8, 64
PIECES = 2
DP = 64 // PIECES
QP = DP // 4
KP = DP * 32


def params(n=1):
    return pltpu.CompilerParams(
        dimension_semantics=("arbitrary",) * n, vmem_limit_bytes=VMEM
    )


def in_hbm(x):
    return pltpu.with_memory_space_constraint(x, pltpu.HBM)


def in_vmem(x):
    return pltpu.with_memory_space_constraint(x, pltpu.VMEM)


def cost(flops, nbytes):
    return pl.CostEstimate(flops=0, bytes_accessed=1024, transcendentals=0)


def after(values, *others):
    return lax.optimization_barrier((tuple(values), tuple(others)))[0]


def lane_swap():
    out = np.zeros((4, 4, 4, 32, 4, 4, 32), np.float32)
    for first in range(4):
        for e in range(4):
            for z in range(4):
                for c in range(32):
                    out[first, e, z, c, (z - first) % 4, e, c] = 1
    return out.reshape(4, 512, 512).astype(jnp.bfloat16)


def pack_kernel(piece, tab_ref, amp_ref, lanes_ref, *rest):
    outs, mid_ref = rest[:4], rest[4]
    for jh in range(2):
        rows = slice(16 * jh, 16 * jh + 16)
        for dh in range(DP // 16):
            y = jnp.swapaxes(amp_ref[0, rows, 16 * dh : 16 * dh + 16, :], 0, 1)
            for x in range(4):
                to = x if piece else (x - tab_ref[4]) & 3
                for q in range(4):
                    for e in range(4):
                        mid_ref[to, 4 * dh + q, rows, 128 * e : 128 * e + 128] = y[
                            4 * q + e, :, 128 * x : 128 * x + 128
                        ]
    w = jnp.dot(mid_ref[...].reshape(4 * QP * OJ, 512), lanes_ref[0], preferred_element_type=F32)
    w = w.astype(BF16).reshape(4, QP, OJ, 512)
    for x in range(4):
        for z in range(4):
            block = w[x, :, :, 128 * z : 128 * z + 128]
            if piece:
                outs[z][x, 0] = block
            else:
                outs[x][z, 0] = block


def pack(amp_t, piece, slots, tab):
    return pl.pallas_call(
        functools.partial(pack_kernel, piece),
        grid_spec=pltpu.PrefetchScalarGridSpec(
            num_scalar_prefetch=1,
            grid=(slots,),
            in_specs=[
                pl.BlockSpec((1, OJ, DP, NV), lambda s, tab: (tab[s], 0, piece, 0)),
                pl.BlockSpec((1, 512, 512), lambda s, tab: (tab[5] * piece, 0, 0)),
            ],
            out_specs=[pl.BlockSpec((4, 1, QP, OJ, 128), lambda s, tab: (0, s, 0, 0, 0))] * 4,
            scratch_shapes=[pltpu.VMEM((4, QP, OJ, 512), BF16)],
        ),
        out_shape=[pltpu.HBM((4, slots, QP, OJ, 128), BF16)] * 4,
        compiler_params=params(),
        cost_estimate=cost(8_000_000_000 // PIECES, 2 * 8 * 2**20 // PIECES),
        name="pack",
    )(tab, in_hbm(amp_t), in_hbm(jnp.asarray(lane_swap())))


def regroup_kernel(count, tab_ref, *refs):
    got, outs, (buf_ref, sems, out_sems) = refs[:4], refs[4:8], refs[8:]

    def copy(n, away, rel):
        src = got[away].at[(tab_ref[2, n] + rel) & 3, tab_ref[1, n]]
        return pltpu.make_async_copy(src, buf_ref.at[rel, n], sems.at[rel, n])

    def ship(rel):
        return pltpu.make_async_copy(buf_ref.at[rel], outs[rel], out_sems.at[rel])

    def start(n, carry):
        for away in range(4):

            @pl.when(tab_ref[0, n] == away)
            def _():
                for rel in range(4):
                    copy(n, away, rel).start()

        return carry

    lax.fori_loop(0, count, start, 0)
    for rel in range(4):

        def arrive(n, carry):
            copy(n, 0, rel).wait()
            return carry

        lax.fori_loop(0, count, arrive, 0)
        ship(rel).start()
    for rel in range(4):
        ship(rel).wait()


def regroup(tab, got):
    count = tab.shape[1]
    hbm = pl.BlockSpec(memory_space=pltpu.HBM)
    return pl.pallas_call(
        functools.partial(regroup_kernel, count),
        in_specs=[pl.BlockSpec(memory_space=pltpu.SMEM)] + [hbm] * 4,
        out_specs=[hbm] * 4,
        out_shape=[pltpu.HBM((count, QP, OJ, 128), BF16)] * 4,
        scratch_shapes=[
            pltpu.VMEM((4, count, QP, OJ, 128), BF16),
            pltpu.SemaphoreType.DMA((4, count)),
            pltpu.SemaphoreType.DMA((4,)),
        ],
        compiler_params=pltpu.CompilerParams(vmem_limit_bytes=VMEM),
        cost_estimate=cost(0, 16 * count * 2**15),
        name="regroup",
    )(tab, *[in_hbm(x) for x in got])


def move(x, n, along_x):
    dx, dz = (n, 0) if along_x else (0, n)
    pairs = [(4 * a + b, 4 * ((a + dx) % 4) + (b + dz) % 4) for a in range(4) for b in range(4)]
    return lax.ppermute(x, "row", pairs)


IN_STEP = 8


def ints_kernel(gtab_ref, v_ref, out_ref):
    for dd in range(IN_STEP // 2):
        for ch in range(2):
            x = v_ref[16 * ch : 16 * ch + 16, 16 * dd : 16 * dd + 16, :]
            y = jnp.swapaxes(x, 0, 1)
            for d in range(2):
                row = 64 * dd + 32 * d + 16 * ch
                for a in range(SA):
                    off = 64 * (a % 2)
                    for t in range(4):
                        tile = y[8 * d + a, :, 128 * t : 128 * t + 128]
                        for e in range(2):
                            part = tile[:, 64 * e : 64 * e + 64]
                            out_ref[0, gtab_ref[a, 2 * t + e], row : row + 16, 64 * a : 64 * a + 64] = part


def arrange_ints(first, pieces, gtab, ints, space):
    steps = DP // IN_STEP
    return pl.pallas_call(
        ints_kernel,
        grid_spec=pltpu.PrefetchScalarGridSpec(
            num_scalar_prefetch=1,
            grid=(steps * pieces,),
            in_specs=[pl.BlockSpec((32, 8 * IN_STEP, NV), lambda s, *_: (0, first * steps + s, 0))],
            out_specs=pl.BlockSpec(
                (1, 8, 32 * IN_STEP, NV), lambda s, *_: (s // steps, 0, s % steps, 0)
            ),
        ),
        out_shape=space((pieces, 8, KP, SA * RUN), BF16),
        compiler_params=params(),
        cost_estimate=cost(0, pieces * 8 * 2**20),
        name="arrange_ints",
    )(gtab, in_hbm(ints))


def two_terms(x):
    hi = x.astype(BF16)
    return hi, (x - hi.astype(F32)).astype(BF16)


def ladder_kernel(where_ref, core_ref, *refs):
    r_refs, ints_refs, (cycle_hbm, pick_ref, drop_ref) = refs[:8], refs[8:10], refs[10:13]
    keep_ref, send_ref, rows_ref, slab_ref, ints_ref, cycle_ref, sum_ref, sems, ints_sems, cycle_sem = refs[13:]
    core = core_ref[0]

    def copy(p, piece, away):
        src = r_refs[4 * piece + away].at[where_ref[2 * piece + 1, p]]
        return pltpu.make_async_copy(src, slab_ref.at[p, piece], sems.at[p, piece])

    def copy_ints(g, piece):
        return pltpu.make_async_copy(ints_refs[piece].at[0, g], ints_ref.at[piece, g], ints_sems.at[piece, g])

    copy_cycle = pltpu.make_async_copy(cycle_hbm, cycle_ref, cycle_sem)

    def start(p, carry):
        for piece in range(PIECES):
            for away in range(4):

                @pl.when(where_ref[2 * piece, p] == away)
                def _():
                    copy(p, piece, away).start()

        return carry

    def sort(blk, carry):
        for i in range(4):
            for piece in range(PIECES):
                copy(4 * blk + i, piece, 0).wait()
        x = jnp.concatenate(
            [
                jnp.concatenate(
                    [slab_ref[4 * blk + i, piece, q] for piece in range(PIECES) for q in range(QP)], axis=1
                )
                for i in range(4)
            ],
            axis=0,
        )
        y = jnp.dot(pick_ref[blk], x, preferred_element_type=F32).astype(BF16)
        rows_ref[:, pl.ds(pl.multiple_of(32 * blk, 32), 32), :] = y.reshape(8, 32, PIECES * KP)
        return carry

    def group(g, carry):
        for piece in range(PIECES):
            copy_ints(g, piece).wait()
        sum_ref[g] = sum(
            jnp.dot(
                rows_ref[g, :, KP * piece : KP * piece + KP], ints_ref[piece, g], preferred_element_type=F32
            )
            for piece in range(PIECES)
        )
        return carry

    def unsort(blk, carry):
        x = sum_ref[:, pl.ds(pl.multiple_of(32 * blk, 32), 32), :].reshape(256, SA * RUN)
        hi, lo = two_terms(x)
        y = jnp.dot(drop_ref[blk], hi, preferred_element_type=F32)
        y = y + jnp.dot(drop_ref[blk], lo, preferred_element_type=F32)
        for i in range(4):
            got = y[32 * i : 32 * i + 32, :] + cycle_ref[4 * blk + i]

            @pl.when(core == i % 2)
            def _():
                keep_ref[2 * blk + i // 2] = got

            @pl.when(core != i % 2)
            def _():
                send_ref[2 * blk + i // 2] = got

        return carry

    lax.fori_loop(0, OI, start, 0)
    for g in range(8):
        for piece in range(PIECES):
            copy_ints(g, piece).start()
    copy_cycle.start()
    lax.fori_loop(0, 8, sort, 0)
    lax.fori_loop(0, 8, group, 0)
    copy_cycle.wait()
    lax.fori_loop(0, 8, unsort, 0)


def ladder(where, core, arrived, pick, early, late, drop, cyc):
    smem = pl.BlockSpec(memory_space=pltpu.SMEM)
    vmem = pl.BlockSpec(memory_space=pltpu.VMEM)
    hbm = pl.BlockSpec(memory_space=pltpu.HBM)
    return pl.pallas_call(
        ladder_kernel,
        in_specs=[smem] * 2 + [hbm] * 11 + [vmem] * 2,
        out_specs=[vmem] * 2,
        out_shape=[jax.ShapeDtypeStruct((16, OJ, 512), F32)] * 2,
        scratch_shapes=[
            pltpu.VMEM((8, 256, PIECES * KP), BF16),
            pltpu.VMEM((OI, PIECES, QP, OJ, 128), BF16),
            pltpu.VMEM((PIECES, 8, KP, 512), BF16),
            pltpu.VMEM((OI, OJ, 512), F32),
            pltpu.VMEM((8, 256, 512), F32),
            pltpu.SemaphoreType.DMA((OI, PIECES)),
            pltpu.SemaphoreType.DMA((PIECES, 8)),
            pltpu.SemaphoreType.DMA(()),
        ],
        compiler_params=pltpu.CompilerParams(vmem_limit_bytes=VMEM),
        cost_estimate=cost(5_400_000_000, 30 * 2**20),
        name="ladder",
    )(where, core, *[in_hbm(x) for x in (*arrived, early, late, cyc)], pick, drop)


def cycle_kernel(ovov_ref, amp_ref, want_ref, sym_ref, out_ref, mid_ref, turn_ref):
    acc = None
    for k in range(4):
        part = lax.dot_general(
            ovov_ref[:, NV * k : NV * k + NV],
            amp_ref[k].reshape(512, NV),
            (((1,), (1,)), ((), ())),
            preferred_element_type=F32,
        )
        acc = part if acc is None else acc + part
    low = lax.broadcasted_iota(jnp.int32, (OI, 128), 1) < 64
    for t in range(4):
        mid_ref[t] = acc[:, 128 * t : 128 * t + 128]
    for t in range(4):
        keep = [
            jnp.broadcast_to(want_ref[2 * t + e], (OI, 128)) for e in range(2)
        ]
        for m in range(4):
            x0 = mid_ref[t, pl.ds(2 * m, OI, stride=SA), :]
            x1 = mid_ref[t, pl.ds(2 * m + 1, OI, stride=SA), :]
            sym = sym_ref[0:1, 128 * m : 128 * m + 128]
            y0 = jnp.where(low, x0, pltpu.roll(x1, 64, 1))
            y1 = jnp.where(low, pltpu.roll(x0, 64, 1), x1)
            turn_ref[m, pl.ds(2 * t, OI, stride=8), :] = jnp.where(keep[0] == sym, y0, 0.0)
            turn_ref[m, pl.ds(2 * t + 1, OI, stride=8), :] = jnp.where(keep[1] == sym, y1, 0.0)
    for m in range(4):
        out_ref[:, :, 128 * m : 128 * m + 128] = turn_ref[m].reshape(OI, 8, 128)


def cycle_term(ovov, amp_t, want, sym):
    return pl.pallas_call(
        cycle_kernel,
        grid=(4,),
        in_specs=[
            pl.BlockSpec((OI * SA, 4 * NV), lambda s: (0, 0)),
            pl.BlockSpec((4, 8, RUN, NV), lambda s: (0, s, 0, 0)),
            pl.BlockSpec((8, OI, 1), lambda s: (s, 0, 0)),
            pl.BlockSpec((8, 512), lambda s: (0, 0)),
        ],
        out_specs=pl.BlockSpec((OI, 8, 512), lambda s: (0, s, 0)),
        out_shape=jax.ShapeDtypeStruct((OI, OJ, 512), F32),
        scratch_shapes=[pltpu.VMEM((4, OI * SA, 128), F32), pltpu.VMEM((4, OI * 8, 128), F32)],
        compiler_params=params(),
        cost_estimate=cost(2_100_000_000, 11 * 2**20),
        name="cycle_term",
    )(in_hbm(ovov), in_hbm(amp_t), want, sym)


def by_run_kernel(ltab_ref, x_ref, spread_ref, out_ref):
    hi, lo = two_terms(jnp.sum(x_ref[...], axis=0))
    y = jnp.dot(spread_ref[...], hi, preferred_element_type=F32)
    y = y + jnp.dot(spread_ref[...], lo, preferred_element_type=F32)
    for a in range(SA):
        for t in range(8):
            out_ref[ltab_ref[a, t], :, 64 * a : 64 * a + 64] = y[8 * t : 8 * t + 8, 64 * a : 64 * a + 64]


def by_run(ltab, x, spread):
    return pl.pallas_call(
        by_run_kernel,
        grid_spec=pltpu.PrefetchScalarGridSpec(
            num_scalar_prefetch=1,
            grid=(1,),
            in_specs=[
                pl.BlockSpec((ROWS, OJ, 512), lambda s, *_: (0, 0, 0)),
                pl.BlockSpec((64, OJ), lambda s, *_: (0, 0)),
            ],
            out_specs=pl.BlockSpec((8, 8, 512), lambda s, *_: (0, 0, 0)),
        ),
        out_shape=jax.ShapeDtypeStruct((8, 8, 512), F32),
        compiler_params=params(),
        name="by_run",
    )(ltab, x, spread)


def finish_kernel(slot_ref, irr_ref, energy_ref, x_ref, va_ref, vb_ref, sa_ref, sb_ref, out_ref, tile_ref):
    for h in range(2):
        v = x_ref[h]
        for y in range(1, 4):
            v = v + x_ref[2 * y + h]
        for a in range(SA):
            tile_ref[h, :, a, :] = v[:, 64 * a : 64 * a + 64]
    sym_ab = jnp.bitwise_xor(sa_ref[...], sb_ref[...])
    for h in range(2):
        for j in range(OJ):
            got = tile_ref[h, slot_ref[j]]
            den = energy_ref[h, j] - va_ref[...] - vb_ref[...]
            ok = jnp.bitwise_xor(sym_ab, irr_ref[h, j]) == 0
            out_ref[h, j] = jnp.where(ok, got / den, jnp.zeros_like(got))


def finish(slot, irr, energy, x, va, vb, sa, sb):
    full = lambda *dims: pl.BlockSpec(dims, lambda s, *_: (0,) * len(dims))
    return pl.pallas_call(
        finish_kernel,
        grid_spec=pltpu.PrefetchScalarGridSpec(
            num_scalar_prefetch=3,
            grid=(1,),
            in_specs=[full(8, 8, 512), full(8, 64), full(8, 64), full(8, 64), full(8, 64)],
            out_specs=full(2, OJ, SA, RUN),
            scratch_shapes=[pltpu.VMEM((2, 8, SA, RUN), F32)],
        ),
        out_shape=jax.ShapeDtypeStruct((2, OJ, SA, RUN), F32),
        compiler_params=params(),
        name="finish",
    )(slot, irr, energy, x, va, vb, sa, sb)


def body(
    slots,
    count,
    amplitudes,
    vvvv_ints,
    ovov_ints,
    occ_energy,
    vir_energy,
    occ_irrep,
    vir_irrep,
    i_orbitals,
    j_orbitals,
    a_orbitals,
):
    row = lax.axis_index("row")
    col = lax.axis_index("col")
    core = lax.rem(col, 2)
    labels = jnp.arange(8, dtype=jnp.int32)
    amp_t = amplitudes.transpose(0, 1, 3, 2)

    x_pos, z_pos = row // 4, row % 4
    lane = jnp.arange(4, dtype=jnp.int32)
    is_i = i_orbitals[:, None] == jnp.arange(NO)
    chosen = is_i.any(axis=0).reshape(4, 4, 4)
    if slots == 4:
        slot_of = jnp.broadcast_to(lane, (4, 4, 4))
        ktab = lane
    else:
        slot_of = jnp.sum(chosen[:, :, None, :] & (lane[:, None] > lane), axis=-1).astype(jnp.int32)
        own = lambda x: lax.dynamic_index_in_dim(x.reshape(ROWS, 4), row, keepdims=False)
        ktab = jnp.sum(jnp.where(own(chosen) & (own(slot_of) == lane[:, None]), lane, 0), axis=-1)
    ptab = jnp.concatenate([ktab, jnp.stack([x_pos, z_pos])]).astype(jnp.int32)
    packed = pack(amp_t, 1, slots, ptab)
    second = {n: move(packed[n], n, False) for n in (1, 3)}
    sent = [pack(amp_t, 0, slots, *after([ptab], packed[0])), packed]
    first = {n: move(sent[0][n], n, True) for n in (1, 3, 2)}

    line_before = jnp.arange(16)[:, None] > jnp.arange(16)
    others = jnp.arange(16, dtype=jnp.int32) // 4
    tabs, where = [], []
    for piece in range(2):
        mine, other = (x_pos, z_pos) if piece else (z_pos, x_pos)
        by_line = lambda x: (x if piece else x.transpose(1, 0, 2)).reshape(4, 16)
        line = by_line(chosen)
        rank = jnp.sum(line[:, None, :] & line_before, axis=-1).astype(jnp.int32)
        here, here_rank, here_slot = [
            lax.dynamic_index_in_dim(x, mine, keepdims=False) for x in (line, rank, by_line(slot_of))
        ]
        nth = here & (here_rank == jnp.arange(count)[:, None])
        nth_other = jnp.sum(jnp.where(nth, others, 0), axis=-1)
        nth_slot = jnp.sum(jnp.where(nth, here_slot, 0), axis=-1)
        tabs.append(jnp.stack([(other - nth_other) & 3, nth_slot, jnp.full_like(nth_slot, mine)]).astype(jnp.int32))
        rank = rank.reshape(4, 4, 4)
        rank = (rank if piece else rank.transpose(1, 0, 2)).reshape(NO)
        away = (mine - (i_orbitals // (16 if piece else 4)) % 4) & 3
        where.append(jnp.stack([away, jnp.sum(jnp.where(is_i, rank, 0), axis=-1)]).astype(jnp.int32))

    sym_i = jnp.take(occ_irrep, i_orbitals)
    sym_j = jnp.take(occ_irrep, j_orbitals)
    sym_a = jnp.take(vir_irrep, a_orbitals)
    run_label = vir_irrep.reshape(8, RUN)[:, 0]
    slot = j_orbitals % 8
    gtab = jnp.bitwise_xor(sym_a[:, None], run_label[None, :])
    g_ij = jnp.bitwise_xor(sym_i[:, None], sym_j[None, :])
    hit = (g_ij[:, :, None, None] == labels[:, None]) & (slot[:, None, None] == labels)
    hit = hit.reshape(8, 4, OJ, 8, 8)
    same = (jnp.arange(4)[:, None] == jnp.arange(4)).reshape(1, 4, 1, 1, 4, 1)
    drop = (hit[:, :, :, :, None, :] & same).reshape(8, 128, 256).astype(BF16)
    pick = drop.transpose(0, 2, 1)
    mine_label = lax.dynamic_index_in_dim(run_label, col, keepdims=False)
    want = jnp.bitwise_xor(g_ij.T, mine_label)[:, :, None]
    sym_lanes = jnp.broadcast_to(jnp.repeat(sym_a, RUN)[None, :], (8, SA * RUN))

    mine_i = lax.dynamic_slice_in_dim(i_orbitals, 2 * row, 2)
    sym_mine = jnp.take(occ_irrep, mine_i)
    label_at = jnp.bitwise_xor(
        jnp.bitwise_xor(lax.dynamic_index_in_dim(sym_mine, core, keepdims=False), sym_a)[:, None],
        labels[None, :],
    )
    ltab = jnp.sum(jnp.where(label_at[..., None] == run_label, labels, 0), axis=-1).astype(jnp.int32)
    spread = (
        (sym_j[None, None, :] == labels[:, None, None]) & (slot[None, None, :] == labels[None, :, None])
    ).reshape(64, OJ).astype(BF16)
    energy = jnp.take(occ_energy, mine_i)[:, None] + jnp.take(occ_energy, j_orbitals)[None, :]
    irr = jnp.bitwise_xor(sym_mine[:, None], sym_j[None, :])
    wide = lambda x: jnp.broadcast_to(x, (SA, RUN))
    va = wide(jnp.take(vir_energy, a_orbitals)[:, None])
    vb = wide(lax.dynamic_slice_in_dim(vir_energy, col * RUN, RUN)[None, :])
    sa = wide(sym_a[:, None])
    sb = wide(lax.dynamic_slice_in_dim(vir_irrep, col * RUN, RUN)[None, :])
    tail = (ltab, spread, slot, irr, energy, va, vb, sa, sb)

    ints = vvvv_ints.reshape(32, 512, NV)
    (held,) = after([sent[1][2]], second[1], second[3])
    second[2] = move(held, 2, False)
    (want,) = after([want], second[1], second[3])
    cyc = cycle_term(ovov_ints.reshape(OI * SA, 4 * NV), amp_t, want, sym_lanes)
    (gate,) = after([gtab], cyc)
    early = arrange_ints(0, 1, gate, ints, pltpu.HBM)
    (tab1,) = after([tabs[1]], early, pick)
    packed1 = regroup(tab1, [sent[1][0], second[1], second[2], second[3]])
    (tab0,) = after([tabs[0]], packed1[0])
    packed0 = regroup(tab0, [sent[0][0], first[1], first[2], first[3]])
    sides1 = after([packed1[1], packed1[3]], first[1], first[2], first[3])
    arrived0 = {n: move(packed0[n], n, False) for n in (1, 3)}
    arrived1 = {n: move(x, n, True) for n, x in zip((1, 3), sides1)}
    (gate,) = after([gtab], packed0[0], *tail)
    late = arrange_ints(1, 1, gate, ints, pltpu.HBM)
    across0, across1 = after(
        [packed0[2], packed1[2]], late, list(arrived0.values()), list(arrived1.values())
    )
    arrived0[2] = move(across0, 2, False)
    arrived1[2] = move(across1, 2, True)
    keep, give = ladder(
        jnp.concatenate(where),
        core.reshape(1),
        [packed0[0], arrived0[1], arrived0[2], arrived0[3], packed1[0], arrived1[1], arrived1[2], arrived1[3]],
        pick, early, late, drop, cyc,
    )

    got = lax.ppermute(give, "col", [(q, q ^ 1) for q in range(COLS)])
    both = lax.all_to_all(keep + got, "row", split_axis=0, concat_axis=0, tiled=True)
    parts = lax.all_to_all(by_run(ltab, both, spread), "col", split_axis=0, concat_axis=0, tiled=True)
    return finish(slot, irr, energy, parts, va, vb, sa, sb)


def shards(*args):
    lines = jnp.stack([args[7] // 16, args[7] // 4 % 4])
    on_line = jnp.max(jnp.sum(lines[:, None, :] == jnp.arange(4)[:, None], axis=-1))
    return lax.cond(
        on_line > 12, functools.partial(body, 4, 16), functools.partial(body, 4, 12), *args
    )


def solution(mesh):
    return jax.shard_map(
        shards,
        mesh=mesh,
        in_specs=(
            P("row", None, None, "col"),
            P("row", "col", None, None),
            P(None, None, "row", None),
            P(),
            P(),
            P(),
            P(),
            P(),
            P(),
            P(),
        ),
        out_specs=P("row", None, None, "col"),
        check_vma=False,
    )
```

```python
import functools

import jax
import jax.numpy as jnp
from jax import lax
from jax.experimental import pallas as pl
from jax.experimental.pallas import tpu as pltpu
from jax.sharding import PartitionSpec as P

F32 = jnp.float32
BF16 = jnp.bfloat16
VMEM = 50 * 1024 * 1024

NO, NV, OI, OJ, SA = 64, 512, 32, 32, 8
ROWS, COLS, RUN = 16, 8, 64
PIECES = 2
DP = 64 // PIECES
QP = DP // 4
KP = DP * 32


def params(n=1):
    return pltpu.CompilerParams(
        dimension_semantics=("arbitrary",) * n, vmem_limit_bytes=VMEM
    )


def in_hbm(x):
    return pltpu.with_memory_space_constraint(x, pltpu.HBM)


def in_vmem(x):
    return pltpu.with_memory_space_constraint(x, pltpu.VMEM)


def cost(flops, nbytes):
    return pl.CostEstimate(flops=0, bytes_accessed=1024, transcendentals=0)


def after(values, *others):
    return lax.optimization_barrier((tuple(values), tuple(others)))[0]


def lane_swap(z):
    src = lax.broadcasted_iota(jnp.int32, (512, 128), 0)
    dst = lax.broadcasted_iota(jnp.int32, (512, 128), 1)
    return (src == (dst & 31) + 32 * z + 128 * (dst >> 5)).astype(F32).astype(BF16)


def pack_kernel(piece, slots, tab_ref, amp_ref, *rest):
    outs, (in_ref, mid_ref, turn_ref, out_ref, in_sems, out_sems) = rest[:4], rest[4:]

    def fetch(slot):
        src = amp_ref.at[tab_ref[slot], :, pl.ds(DP * piece, DP), :]
        return pltpu.make_async_copy(src, in_ref.at[slot], in_sems.at[slot])

    def ship(slot, n):
        return pltpu.make_async_copy(out_ref.at[slot, n], outs[n].at[:, slot], out_sems.at[slot, n])

    for slot in range(slots):
        fetch(slot).start()
    for z in range(4):
        turn_ref[:, 128 * z : 128 * z + 128] = lane_swap((z + tab_ref[5]) & 3 if piece else z)

    def work(slot, carry):
        fetch(slot).wait()
        for jh in range(2):
            rows = slice(16 * jh, 16 * jh + 16)
            for dh in range(DP // 16):
                y = jnp.swapaxes(in_ref[slot, rows, 16 * dh : 16 * dh + 16, :], 0, 1)
                for x in range(4):
                    for q in range(4):
                        for e in range(4):
                            mid_ref[x, 4 * dh + q, rows, 128 * e : 128 * e + 128] = y[
                                4 * q + e, :, 128 * x : 128 * x + 128
                            ]
        w = jnp.dot(mid_ref[...].reshape(4 * QP * OJ, 512), turn_ref[...], preferred_element_type=F32)
        w = w.astype(BF16).reshape(4, QP, OJ, 512)
        for x in range(4):
            for z in range(4):
                block = w[x, :, :, 128 * z : 128 * z + 128]
                if piece:
                    out_ref[slot, z, x] = block
                else:
                    out_ref[slot, (x - tab_ref[4]) & 3, z] = block
        for n in range(4):
            ship(slot, n).start()
        return carry

    lax.fori_loop(0, slots, work, 0)
    for slot in range(slots):
        for n in range(4):
            ship(slot, n).wait()


def pack(amp_t, piece, slots, tab):
    hbm = pl.BlockSpec(memory_space=pltpu.HBM)
    return pl.pallas_call(
        functools.partial(pack_kernel, piece, slots),
        in_specs=[pl.BlockSpec(memory_space=pltpu.SMEM), hbm],
        out_specs=[hbm] * 4,
        out_shape=[pltpu.HBM((4, slots, QP, OJ, 128), BF16)] * 4,
        scratch_shapes=[
            pltpu.VMEM((slots, OJ, DP, NV), BF16),
            pltpu.VMEM((4, QP, OJ, 512), BF16),
            pltpu.VMEM((512, 512), BF16),
            pltpu.VMEM((slots, 4, 4, QP, OJ, 128), BF16),
            pltpu.SemaphoreType.DMA((slots,)),
            pltpu.SemaphoreType.DMA((slots, 4)),
        ],
        compiler_params=pltpu.CompilerParams(vmem_limit_bytes=VMEM),
        cost_estimate=cost(8_000_000_000 // PIECES, 2 * 8 * 2**20 // PIECES),
        name="pack",
    )(tab, in_hbm(amp_t))


def regroup_kernel(count, rels, tab_ref, *refs):
    got, outs, (buf_ref, sems, out_sems) = refs[:4], refs[4:6], refs[6:]

    def copy(n, away, at):
        src = got[away].at[(tab_ref[2, n] + rels[at]) & 3, tab_ref[1, n]]
        return pltpu.make_async_copy(src, buf_ref.at[at, n], sems.at[at, n])

    def ship(at):
        return pltpu.make_async_copy(buf_ref.at[at], outs[at], out_sems.at[at])

    def start(n, carry):
        for away in range(4):

            @pl.when(tab_ref[0, n] == away)
            def _():
                for at in range(2):
                    copy(n, away, at).start()

        return carry

    lax.fori_loop(0, count, start, 0)
    for at in range(2):

        def arrive(n, carry):
            copy(n, 0, at).wait()
            return carry

        lax.fori_loop(0, count, arrive, 0)
        ship(at).start()
    for at in range(2):
        ship(at).wait()


def regroup(tab, got, *rels):
    count = tab.shape[1]
    hbm = pl.BlockSpec(memory_space=pltpu.HBM)
    return pl.pallas_call(
        functools.partial(regroup_kernel, count, rels),
        in_specs=[pl.BlockSpec(memory_space=pltpu.SMEM)] + [hbm] * 4,
        out_specs=[hbm] * 2,
        out_shape=[pltpu.HBM((count, QP, OJ, 128), BF16)] * 2,
        scratch_shapes=[
            pltpu.VMEM((2, count, QP, OJ, 128), BF16),
            pltpu.SemaphoreType.DMA((2, count)),
            pltpu.SemaphoreType.DMA((2,)),
        ],
        compiler_params=pltpu.CompilerParams(vmem_limit_bytes=VMEM),
        cost_estimate=cost(0, 8 * count * 2**15),
        name="regroup",
    )(tab, *[in_hbm(x) for x in got])


def move(x, n, along_x):
    dx, dz = (n, 0) if along_x else (0, n)
    pairs = [(4 * a + b, 4 * ((a + dx) % 4) + (b + dz) % 4) for a in range(4) for b in range(4)]
    return lax.ppermute(x, "row", pairs)


IN_STEP = 8


def ints_kernel(gtab_ref, v_ref, out_ref):
    for dd in range(IN_STEP // 2):
        for ch in range(2):
            x = v_ref[16 * ch : 16 * ch + 16, 16 * dd : 16 * dd + 16, :]
            y = jnp.swapaxes(x, 0, 1)
            for d in range(2):
                row = 64 * dd + 32 * d + 16 * ch
                for a in range(SA):
                    off = 64 * (a % 2)
                    for t in range(4):
                        tile = y[8 * d + a, :, 128 * t : 128 * t + 128]
                        for e in range(2):
                            part = tile[:, 64 * e : 64 * e + 64]
                            out_ref[0, gtab_ref[a, 2 * t + e], row : row + 16, 64 * a : 64 * a + 64] = part


def arrange_ints(first, pieces, gtab, ints, space):
    steps = DP // IN_STEP
    return pl.pallas_call(
        ints_kernel,
        grid_spec=pltpu.PrefetchScalarGridSpec(
            num_scalar_prefetch=1,
            grid=(steps * pieces,),
            in_specs=[pl.BlockSpec((32, 8 * IN_STEP, NV), lambda s, *_: (0, first * steps + s, 0))],
            out_specs=pl.BlockSpec(
                (1, 8, 32 * IN_STEP, NV), lambda s, *_: (s // steps, 0, s % steps, 0)
            ),
        ),
        out_shape=space((pieces, 8, KP, SA * RUN), BF16),
        compiler_params=params(),
        cost_estimate=cost(0, pieces * 8 * 2**20),
        name="arrange_ints",
    )(gtab, in_hbm(ints))


def two_terms(x):
    hi = x.astype(BF16)
    return hi, (x - hi.astype(F32)).astype(BF16)


def ladder_kernel(where_ref, core_ref, *refs):
    r_refs, ints_hbm, small_hbm = refs[:8], refs[8:10], refs[10:13]
    keep_ref, send_ref, rows_ref, slab_ref, ints_ref, sum_ref = refs[13:19]
    small_refs, sems, ints_sems, small_sems = refs[19:22], *refs[22:]
    pick_ref, drop_ref, cycle_ref = small_refs
    core = core_ref[0]

    def copy(p, piece, away):
        src = r_refs[4 * piece + away].at[where_ref[2 * piece + 1, p]]
        return pltpu.make_async_copy(src, slab_ref.at[p, piece], sems.at[p, piece])

    def copy_ints(g, piece):
        dst = ints_ref.at[g, pl.ds(KP * piece, KP)]
        return pltpu.make_async_copy(ints_hbm[piece].at[0, g], dst, ints_sems.at[piece, g])

    def copy_small(n):
        return pltpu.make_async_copy(small_hbm[n], small_refs[n], small_sems.at[n])

    def start(p, carry):
        for piece in range(PIECES):
            for away in range(4):

                @pl.when(where_ref[2 * piece, p] == away)
                def _():
                    copy(p, piece, away).start()

        return carry

    def sort(blk, carry):
        for i in range(4):
            for piece in range(PIECES):
                copy(4 * blk + i, piece, 0).wait()
        x = jnp.concatenate(
            [
                jnp.concatenate(
                    [slab_ref[4 * blk + i, piece, q] for piece in range(PIECES) for q in range(QP)], axis=1
                )
                for i in range(4)
            ],
            axis=0,
        )
        y = jnp.dot(pick_ref[blk], x, preferred_element_type=F32).astype(BF16)
        rows_ref[:, pl.ds(pl.multiple_of(32 * blk, 32), 32), :] = y.reshape(8, 32, PIECES * KP)
        return carry

    def group(g, carry):
        for piece in range(PIECES):
            copy_ints(g, piece).wait()
        sum_ref[g] = sum(
            jnp.dot(
                rows_ref[g, :, KP * piece : KP * piece + KP],
                ints_ref[g, KP * piece : KP * piece + KP],
                preferred_element_type=F32,
            )
            for piece in range(PIECES)
        )
        return carry

    def unsort(blk, carry):
        x = sum_ref[:, pl.ds(pl.multiple_of(32 * blk, 32), 32), :].reshape(256, SA * RUN)
        hi, lo = two_terms(x)
        y = jnp.dot(drop_ref[blk], hi, preferred_element_type=F32)
        y = y + jnp.dot(drop_ref[blk], lo, preferred_element_type=F32)
        for i in range(4):
            got = y[32 * i : 32 * i + 32, :] + cycle_ref[4 * blk + i]

            @pl.when(core == i % 2)
            def _():
                keep_ref[2 * blk + i // 2] = got

            @pl.when(core != i % 2)
            def _():
                send_ref[2 * blk + i // 2] = got

        return carry

    copy_small(0).start()
    lax.fori_loop(0, OI, start, 0)
    for g in range(8):
        for piece in range(PIECES):
            copy_ints(g, piece).start()
    for n in (1, 2):
        copy_small(n).start()
    copy_small(0).wait()
    lax.fori_loop(0, 8, sort, 0)
    lax.fori_loop(0, 8, group, 0)
    for n in (1, 2):
        copy_small(n).wait()
    lax.fori_loop(0, 8, unsort, 0)


def ladder(where, core, arrived, pick, early, late, drop, cyc):
    smem = pl.BlockSpec(memory_space=pltpu.SMEM)
    vmem = pl.BlockSpec(memory_space=pltpu.VMEM)
    hbm = pl.BlockSpec(memory_space=pltpu.HBM)
    return pl.pallas_call(
        ladder_kernel,
        in_specs=[smem] * 2 + [hbm] * 13,
        out_specs=[vmem] * 2,
        out_shape=[jax.ShapeDtypeStruct((16, OJ, 512), F32)] * 2,
        scratch_shapes=[
            pltpu.VMEM((8, 256, PIECES * KP), BF16),
            pltpu.VMEM((OI, PIECES, QP, OJ, 128), BF16),
            pltpu.VMEM((8, PIECES * KP, 512), BF16),
            pltpu.VMEM((8, 256, 512), F32),
            pltpu.VMEM((8, 256, 128), BF16),
            pltpu.VMEM((8, 128, 256), BF16),
            pltpu.VMEM((OI, OJ, 512), F32),
            pltpu.SemaphoreType.DMA((OI, PIECES)),
            pltpu.SemaphoreType.DMA((PIECES, 8)),
            pltpu.SemaphoreType.DMA((3,)),
        ],
        compiler_params=pltpu.CompilerParams(vmem_limit_bytes=VMEM),
        cost_estimate=cost(5_400_000_000, 30 * 2**20),
        name="ladder",
    )(where, core, *[in_hbm(x) for x in (*arrived, early, late, pick, drop, cyc)])


def cycle_kernel(ovov_ref, amp_ref, want_ref, sym_ref, out_ref, mid_ref, turn_ref):
    acc = None
    for k in range(4):
        part = lax.dot_general(
            ovov_ref[:, NV * k : NV * k + NV],
            amp_ref[k].reshape(512, NV),
            (((1,), (1,)), ((), ())),
            preferred_element_type=F32,
        )
        acc = part if acc is None else acc + part
    low = lax.broadcasted_iota(jnp.int32, (OI, 128), 1) < 64
    for t in range(4):
        mid_ref[t] = acc[:, 128 * t : 128 * t + 128]
    for t in range(4):
        keep = [
            jnp.broadcast_to(want_ref[2 * t + e], (OI, 128)) for e in range(2)
        ]
        for m in range(4):
            x0 = mid_ref[t, pl.ds(2 * m, OI, stride=SA), :]
            x1 = mid_ref[t, pl.ds(2 * m + 1, OI, stride=SA), :]
            sym = sym_ref[0:1, 128 * m : 128 * m + 128]
            y0 = jnp.where(low, x0, pltpu.roll(x1, 64, 1))
            y1 = jnp.where(low, pltpu.roll(x0, 64, 1), x1)
            turn_ref[m, pl.ds(2 * t, OI, stride=8), :] = jnp.where(keep[0] == sym, y0, 0.0)
            turn_ref[m, pl.ds(2 * t + 1, OI, stride=8), :] = jnp.where(keep[1] == sym, y1, 0.0)
    for m in range(4):
        out_ref[:, :, 128 * m : 128 * m + 128] = turn_ref[m].reshape(OI, 8, 128)


def cycle_term(ovov, amp_t, want, sym):
    return pl.pallas_call(
        cycle_kernel,
        grid=(4,),
        in_specs=[
            pl.BlockSpec((OI * SA, 4 * NV), lambda s: (0, 0)),
            pl.BlockSpec((4, 8, RUN, NV), lambda s: (0, s, 0, 0)),
            pl.BlockSpec((8, OI, 1), lambda s: (s, 0, 0)),
            pl.BlockSpec((8, 512), lambda s: (0, 0)),
        ],
        out_specs=pl.BlockSpec((OI, 8, 512), lambda s: (0, s, 0)),
        out_shape=jax.ShapeDtypeStruct((OI, OJ, 512), F32),
        scratch_shapes=[pltpu.VMEM((4, OI * SA, 128), F32), pltpu.VMEM((4, OI * 8, 128), F32)],
        compiler_params=params(),
        cost_estimate=cost(2_100_000_000, 11 * 2**20),
        name="cycle_term",
    )(in_hbm(ovov), in_hbm(amp_t), want, sym)


def by_run_kernel(ltab_ref, x_ref, spread_ref, out_ref):
    hi, lo = two_terms(jnp.sum(x_ref[...], axis=0))
    y = jnp.dot(spread_ref[...], hi, preferred_element_type=F32)
    y = y + jnp.dot(spread_ref[...], lo, preferred_element_type=F32)
    for a in range(SA):
        for t in range(8):
            out_ref[ltab_ref[a, t], :, 64 * a : 64 * a + 64] = y[8 * t : 8 * t + 8, 64 * a : 64 * a + 64]


def by_run(ltab, x, spread):
    return pl.pallas_call(
        by_run_kernel,
        grid_spec=pltpu.PrefetchScalarGridSpec(
            num_scalar_prefetch=1,
            grid=(1,),
            in_specs=[
                pl.BlockSpec((ROWS, OJ, 512), lambda s, *_: (0, 0, 0)),
                pl.BlockSpec((64, OJ), lambda s, *_: (0, 0)),
            ],
            out_specs=pl.BlockSpec((8, 8, 512), lambda s, *_: (0, 0, 0)),
        ),
        out_shape=jax.ShapeDtypeStruct((8, 8, 512), F32),
        compiler_params=params(),
        name="by_run",
    )(ltab, x, spread)


def finish_kernel(slot_ref, irr_ref, energy_ref, x_ref, va_ref, vb_ref, sa_ref, sb_ref, out_ref, tile_ref):
    for h in range(2):
        v = x_ref[h]
        for y in range(1, 4):
            v = v + x_ref[2 * y + h]
        for a in range(SA):
            tile_ref[h, :, a, :] = v[:, 64 * a : 64 * a + 64]
    sym_ab = jnp.bitwise_xor(sa_ref[...], sb_ref[...])
    for h in range(2):
        for j in range(OJ):
            got = tile_ref[h, slot_ref[j]]
            den = energy_ref[h, j] - va_ref[...] - vb_ref[...]
            ok = jnp.bitwise_xor(sym_ab, irr_ref[h, j]) == 0
            out_ref[h, j] = jnp.where(ok, got / den, jnp.zeros_like(got))


def finish(slot, irr, energy, x, va, vb, sa, sb):
    full = lambda *dims: pl.BlockSpec(dims, lambda s, *_: (0,) * len(dims))
    return pl.pallas_call(
        finish_kernel,
        grid_spec=pltpu.PrefetchScalarGridSpec(
            num_scalar_prefetch=3,
            grid=(1,),
            in_specs=[full(8, 8, 512), full(8, 64), full(8, 64), full(8, 64), full(8, 64)],
            out_specs=full(2, OJ, SA, RUN),
            scratch_shapes=[pltpu.VMEM((2, 8, SA, RUN), F32)],
        ),
        out_shape=pltpu.HBM((2, OJ, SA, RUN), F32),
        compiler_params=params(),
        name="finish",
    )(slot, irr, energy, x, va, vb, sa, sb)


def body(
    slots,
    count,
    amplitudes,
    vvvv_ints,
    ovov_ints,
    occ_energy,
    vir_energy,
    occ_irrep,
    vir_irrep,
    i_orbitals,
    j_orbitals,
    a_orbitals,
):
    row = lax.axis_index("row")
    col = lax.axis_index("col")
    core = lax.rem(col, 2)
    labels = jnp.arange(8, dtype=jnp.int32)
    amp_t = amplitudes.transpose(0, 1, 3, 2)

    x_pos, z_pos = row // 4, row % 4
    lane = jnp.arange(4, dtype=jnp.int32)
    is_i = i_orbitals[:, None] == jnp.arange(NO)
    chosen = is_i.any(axis=0).reshape(4, 4, 4)
    if slots == 4:
        slot_of = jnp.broadcast_to(lane, (4, 4, 4))
        ktab = lane
    else:
        slot_of = jnp.sum(chosen[:, :, None, :] & (lane[:, None] > lane), axis=-1).astype(jnp.int32)
        own = lambda x: lax.dynamic_index_in_dim(x.reshape(ROWS, 4), row, keepdims=False)
        ktab = jnp.sum(jnp.where(own(chosen) & (own(slot_of) == lane[:, None]), lane, 0), axis=-1)
    ptab = jnp.concatenate([ktab, jnp.stack([x_pos, z_pos])]).astype(jnp.int32)
    packed = pack(amp_t, 1, slots, ptab)
    second = {n: move(packed[n], n, False) for n in (1, 3)}
    sent = [pack(amp_t, 0, slots, *after([ptab], packed[0])), packed]
    first = {n: move(sent[0][n], n, True) for n in (1, 3, 2)}

    line_before = jnp.arange(16)[:, None] > jnp.arange(16)
    others = jnp.arange(16, dtype=jnp.int32) // 4
    tabs, where = [], []
    for piece in range(2):
        mine, other = (x_pos, z_pos) if piece else (z_pos, x_pos)
        by_line = lambda x: (x if piece else x.transpose(1, 0, 2)).reshape(4, 16)
        line = by_line(chosen)
        rank = jnp.sum(line[:, None, :] & line_before, axis=-1).astype(jnp.int32)
        here, here_rank, here_slot = [
            lax.dynamic_index_in_dim(x, mine, keepdims=False) for x in (line, rank, by_line(slot_of))
        ]
        nth = here & (here_rank == jnp.arange(count)[:, None])
        nth_other = jnp.sum(jnp.where(nth, others, 0), axis=-1)
        nth_slot = jnp.sum(jnp.where(nth, here_slot, 0), axis=-1)
        tabs.append(jnp.stack([(other - nth_other) & 3, nth_slot, jnp.full_like(nth_slot, mine)]).astype(jnp.int32))
        rank = rank.reshape(4, 4, 4)
        rank = (rank if piece else rank.transpose(1, 0, 2)).reshape(NO)
        away = (mine - (i_orbitals // (16 if piece else 4)) % 4) & 3
        where.append(jnp.stack([away, jnp.sum(jnp.where(is_i, rank, 0), axis=-1)]).astype(jnp.int32))

    sym_i = jnp.take(occ_irrep, i_orbitals)
    sym_j = jnp.take(occ_irrep, j_orbitals)
    sym_a = jnp.take(vir_irrep, a_orbitals)
    run_label = vir_irrep.reshape(8, RUN)[:, 0]
    slot = j_orbitals % 8
    gtab = jnp.bitwise_xor(sym_a[:, None], run_label[None, :])
    g_ij = jnp.bitwise_xor(sym_i[:, None], sym_j[None, :])
    hit = (g_ij[:, :, None, None] == labels[:, None]) & (slot[:, None, None] == labels)
    hit = hit.reshape(8, 4, OJ, 8, 8)
    same = (jnp.arange(4)[:, None] == jnp.arange(4)).reshape(1, 4, 1, 1, 4, 1)
    drop = (hit[:, :, :, :, None, :] & same).reshape(8, 128, 256).astype(BF16)
    pick = drop.transpose(0, 2, 1)
    mine_label = lax.dynamic_index_in_dim(run_label, col, keepdims=False)
    want = jnp.bitwise_xor(g_ij.T, mine_label)[:, :, None]
    sym_lanes = jnp.broadcast_to(jnp.repeat(sym_a, RUN)[None, :], (8, SA * RUN))

    mine_i = lax.dynamic_slice_in_dim(i_orbitals, 2 * row, 2)
    sym_mine = jnp.take(occ_irrep, mine_i)
    label_at = jnp.bitwise_xor(
        jnp.bitwise_xor(lax.dynamic_index_in_dim(sym_mine, core, keepdims=False), sym_a)[:, None],
        labels[None, :],
    )
    ltab = jnp.sum(jnp.where(label_at[..., None] == run_label, labels, 0), axis=-1).astype(jnp.int32)
    spread = (
        (sym_j[None, None, :] == labels[:, None, None]) & (slot[None, None, :] == labels[None, :, None])
    ).reshape(64, OJ).astype(BF16)
    energy = jnp.take(occ_energy, mine_i)[:, None] + jnp.take(occ_energy, j_orbitals)[None, :]
    irr = jnp.bitwise_xor(sym_mine[:, None], sym_j[None, :])
    wide = lambda x: jnp.broadcast_to(x, (SA, RUN))
    va = wide(jnp.take(vir_energy, a_orbitals)[:, None])
    vb = wide(lax.dynamic_slice_in_dim(vir_energy, col * RUN, RUN)[None, :])
    sa = wide(sym_a[:, None])
    sb = wide(lax.dynamic_slice_in_dim(vir_irrep, col * RUN, RUN)[None, :])
    tail = (ltab, spread, slot, irr, energy, va, vb, sa, sb)

    ints = vvvv_ints.reshape(32, 512, NV)
    (held,) = after([sent[1][2]], second[1], second[3])
    second[2] = move(held, 2, False)
    (want,) = after([want], second[1], second[3])
    cyc = cycle_term(ovov_ints.reshape(OI * SA, 4 * NV), amp_t, want, sym_lanes)
    (gate,) = after([gtab], cyc)
    early = arrange_ints(0, 1, gate, ints, pltpu.HBM)
    (tab1,) = after([tabs[1]], early, pick)
    lines1 = [sent[1][0], second[1], second[2], second[3]]
    sides1 = regroup(tab1, lines1, 1, 3)
    (tab0,) = after([tabs[0]], sides1)
    lines0 = [sent[0][0], first[1], first[2], first[3]]
    sides0 = regroup(tab0, lines0, 1, 3)
    arrived0 = {n: move(x, n, False) for n, x in zip((1, 3), sides0)}
    sides1 = after(sides1, first[1], first[2], first[3])
    arrived1 = {n: move(x, n, True) for n, x in zip((1, 3), sides1)}
    rest1, rest0 = after([tab1, tab0], sides0)
    across1, arrived1[0] = regroup(rest1, lines1, 2, 0)
    across0, arrived0[0] = regroup(rest0, lines0, 2, 0)
    (across1,) = after([across1], arrived1[1], arrived1[3])
    (across0,) = after([across0], arrived0[1], arrived0[3], across1)
    (gate,) = after([gtab], across0, *tail)
    arrived1[2] = move(across1, 2, True)
    arrived0[2] = move(across0, 2, False)
    late = arrange_ints(1, 1, gate, ints, pltpu.HBM)
    keep, give = ladder(
        jnp.concatenate(where),
        core.reshape(1),
        [arrived0[n] for n in range(4)] + [arrived1[n] for n in range(4)],
        pick, early, late, drop, cyc,
    )

    got = lax.ppermute(give, "col", [(q, q ^ 1) for q in range(COLS)])
    both = lax.all_to_all(keep + got, "row", split_axis=0, concat_axis=0, tiled=True)
    parts = lax.all_to_all(by_run(ltab, both, spread), "col", split_axis=0, concat_axis=0, tiled=True)
    return finish(slot, irr, energy, parts, va, vb, sa, sb)


def shards(*args):
    spots = jnp.stack([args[7] // 16, args[7] // 4 % 4])
    on_line = jnp.max(jnp.sum(spots[:, None, :] == jnp.arange(4)[:, None], axis=-1))
    return lax.cond(
        on_line > 12, functools.partial(body, 4, 16), functools.partial(body, 4, 12), *args
    )


def solution(mesh):
    return jax.shard_map(
        shards,
        mesh=mesh,
        in_specs=(
            P("row", None, None, "col"),
            P("row", "col", None, None),
            P(None, None, "row", None),
            P(),
            P(),
            P(),
            P(),
            P(),
            P(),
            P(),
        ),
        out_specs=P("row", None, None, "col"),
        check_vma=False,
    )
```

```python
import functools

import jax
import jax.numpy as jnp
from jax import lax
from jax.experimental import pallas as pl
from jax.experimental.pallas import tpu as pltpu
from jax.sharding import PartitionSpec as P

F32 = jnp.float32
BF16 = jnp.bfloat16
VMEM = 50 * 1024 * 1024

NO, NV, OI, OJ, SA = 64, 512, 32, 32, 8
ROWS, COLS, RUN = 16, 8, 64
PIECES = 2
DP = 64 // PIECES
QP = DP // 4
KP = DP * 32


def params(n=1):
    return pltpu.CompilerParams(
        dimension_semantics=("arbitrary",) * n, vmem_limit_bytes=VMEM
    )


def in_hbm(x):
    return pltpu.with_memory_space_constraint(x, pltpu.HBM)


def in_vmem(x):
    return pltpu.with_memory_space_constraint(x, pltpu.VMEM)


def cost(flops, nbytes):
    return pl.CostEstimate(flops=0, bytes_accessed=1024, transcendentals=0)


def after(values, *others):
    return lax.optimization_barrier((tuple(values), tuple(others)))[0]


def lane_swap(z):
    src = lax.broadcasted_iota(jnp.int32, (512, 128), 0)
    dst = lax.broadcasted_iota(jnp.int32, (512, 128), 1)
    return (src == (dst & 31) + 32 * z + 128 * (dst >> 5)).astype(F32).astype(BF16)


def pack_kernel(piece, slots, tab_ref, amp_ref, *rest):
    outs, (in_ref, mid_ref, turn_ref, out_ref, in_sems, out_sems) = rest[:4], rest[4:]

    def fetch(slot):
        src = amp_ref.at[tab_ref[slot], :, pl.ds(DP * piece, DP), :]
        return pltpu.make_async_copy(src, in_ref.at[slot], in_sems.at[slot])

    def ship(slot, n):
        return pltpu.make_async_copy(out_ref.at[slot, n], outs[n].at[:, slot], out_sems.at[slot, n])

    for slot in range(slots):
        fetch(slot).start()
    for z in range(4):
        turn_ref[:, 128 * z : 128 * z + 128] = lane_swap((z + tab_ref[5]) & 3 if piece else z)

    def work(slot, carry):
        fetch(slot).wait()
        for jh in range(2):
            rows = slice(16 * jh, 16 * jh + 16)
            for dh in range(DP // 16):
                y = jnp.swapaxes(in_ref[slot, rows, 16 * dh : 16 * dh + 16, :], 0, 1)
                for x in range(4):
                    for q in range(4):
                        for e in range(4):
                            mid_ref[x, 4 * dh + q, rows, 128 * e : 128 * e + 128] = y[
                                4 * q + e, :, 128 * x : 128 * x + 128
                            ]
        w = jnp.dot(mid_ref[...].reshape(4 * QP * OJ, 512), turn_ref[...], preferred_element_type=F32)
        w = w.astype(BF16).reshape(4, QP, OJ, 512)
        for x in range(4):
            for z in range(4):
                block = w[x, :, :, 128 * z : 128 * z + 128]
                if piece:
                    out_ref[slot, z, x] = block
                else:
                    out_ref[slot, (x - tab_ref[4]) & 3, z] = block
        for n in range(4):
            ship(slot, n).start()
        return carry

    lax.fori_loop(0, slots, work, 0)
    for slot in range(slots):
        for n in range(4):
            ship(slot, n).wait()


def pack(amp_t, piece, slots, tab):
    hbm = pl.BlockSpec(memory_space=pltpu.HBM)
    return pl.pallas_call(
        functools.partial(pack_kernel, piece, slots),
        in_specs=[pl.BlockSpec(memory_space=pltpu.SMEM), hbm],
        out_specs=[hbm] * 4,
        out_shape=[pltpu.HBM((4, slots, QP, OJ, 128), BF16)] * 4,
        scratch_shapes=[
            pltpu.VMEM((slots, OJ, DP, NV), BF16),
            pltpu.VMEM((4, QP, OJ, 512), BF16),
            pltpu.VMEM((512, 512), BF16),
            pltpu.VMEM((slots, 4, 4, QP, OJ, 128), BF16),
            pltpu.SemaphoreType.DMA((slots,)),
            pltpu.SemaphoreType.DMA((slots, 4)),
        ],
        compiler_params=pltpu.CompilerParams(vmem_limit_bytes=VMEM),
        cost_estimate=cost(8_000_000_000 // PIECES, 2 * 8 * 2**20 // PIECES),
        name="pack",
    )(tab, in_hbm(amp_t))


def regroup_kernel(count, rels, tab_ref, *refs):
    got, outs, (buf_ref, sems, out_sems) = refs[:4], refs[4:-3], refs[-3:]

    def copy(n, away, at):
        src = got[away].at[(tab_ref[2, n] + rels[at]) & 3, tab_ref[1, n]]
        return pltpu.make_async_copy(src, buf_ref.at[at, n], sems.at[at, n])

    def ship(at):
        return pltpu.make_async_copy(buf_ref.at[at], outs[at], out_sems.at[at])

    def start(n, carry):
        for away in range(4):

            @pl.when(tab_ref[0, n] == away)
            def _():
                for at in range(len(rels)):
                    copy(n, away, at).start()

        return carry

    lax.fori_loop(0, count, start, 0)
    for at in range(len(rels)):

        def arrive(n, carry):
            copy(n, 0, at).wait()
            return carry

        lax.fori_loop(0, count, arrive, 0)
        ship(at).start()
    for at in range(len(rels)):
        ship(at).wait()


def regroup(tab, got, *rels):
    count = tab.shape[1]
    hbm = pl.BlockSpec(memory_space=pltpu.HBM)
    return pl.pallas_call(
        functools.partial(regroup_kernel, count, rels),
        in_specs=[pl.BlockSpec(memory_space=pltpu.SMEM)] + [hbm] * 4,
        out_specs=[hbm] * len(rels),
        out_shape=[pltpu.HBM((count, QP, OJ, 128), BF16)] * len(rels),
        scratch_shapes=[
            pltpu.VMEM((len(rels), count, QP, OJ, 128), BF16),
            pltpu.SemaphoreType.DMA((len(rels), count)),
            pltpu.SemaphoreType.DMA((len(rels),)),
        ],
        compiler_params=pltpu.CompilerParams(vmem_limit_bytes=VMEM),
        cost_estimate=cost(0, 8 * count * 2**15),
        name="regroup",
    )(tab, *[in_hbm(x) for x in got])


def move(x, n, along_x):
    dx, dz = (n, 0) if along_x else (0, n)
    pairs = [(4 * a + b, 4 * ((a + dx) % 4) + (b + dz) % 4) for a in range(4) for b in range(4)]
    return lax.ppermute(x, "row", pairs)


IN_STEP = 8


def ints_kernel(gtab_ref, v_ref, out_ref):
    for dd in range(IN_STEP // 2):
        for ch in range(2):
            x = v_ref[16 * ch : 16 * ch + 16, 16 * dd : 16 * dd + 16, :]
            y = jnp.swapaxes(x, 0, 1)
            for d in range(2):
                row = 64 * dd + 32 * d + 16 * ch
                for a in range(SA):
                    off = 64 * (a % 2)
                    for t in range(4):
                        tile = y[8 * d + a, :, 128 * t : 128 * t + 128]
                        for e in range(2):
                            part = tile[:, 64 * e : 64 * e + 64]
                            out_ref[0, gtab_ref[a, 2 * t + e], row : row + 16, 64 * a : 64 * a + 64] = part


def arrange_ints(first, pieces, gtab, ints, space):
    steps = DP // IN_STEP
    return pl.pallas_call(
        ints_kernel,
        grid_spec=pltpu.PrefetchScalarGridSpec(
            num_scalar_prefetch=1,
            grid=(steps * pieces,),
            in_specs=[pl.BlockSpec((32, 8 * IN_STEP, NV), lambda s, *_: (0, first * steps + s, 0))],
            out_specs=pl.BlockSpec(
                (1, 8, 32 * IN_STEP, NV), lambda s, *_: (s // steps, 0, s % steps, 0)
            ),
        ),
        out_shape=space((pieces, 8, KP, SA * RUN), BF16),
        compiler_params=params(),
        cost_estimate=cost(0, pieces * 8 * 2**20),
        name="arrange_ints",
    )(gtab, in_hbm(ints))


def two_terms(x):
    hi = x.astype(BF16)
    return hi, (x - hi.astype(F32)).astype(BF16)


def ladder_kernel(where_ref, core_ref, *refs):
    r_refs, ints_hbm, small_hbm = refs[:8], refs[8:10], refs[10:13]
    keep_ref, send_ref, rows_ref, slab_ref, ints_ref, sum_ref = refs[13:19]
    small_refs, sems, ints_sems, small_sems = refs[19:22], *refs[22:]
    pick_ref, drop_ref, cycle_ref = small_refs
    core = core_ref[0]

    def copy(p, piece, away):
        src = r_refs[4 * piece + away].at[where_ref[2 * piece + 1, p]]
        return pltpu.make_async_copy(src, slab_ref.at[p, piece], sems.at[p, piece])

    def copy_ints(g, piece):
        dst = ints_ref.at[g, pl.ds(KP * piece, KP)]
        return pltpu.make_async_copy(ints_hbm[piece].at[0, g], dst, ints_sems.at[piece, g])

    def copy_small(n):
        return pltpu.make_async_copy(small_hbm[n], small_refs[n], small_sems.at[n])

    def start(p, carry):
        for piece in range(PIECES):
            for away in range(4):

                @pl.when(where_ref[2 * piece, p] == away)
                def _():
                    copy(p, piece, away).start()

        return carry

    def sort(blk, carry):
        for i in range(4):
            for piece in range(PIECES):
                copy(4 * blk + i, piece, 0).wait()
        x = jnp.concatenate(
            [
                jnp.concatenate(
                    [slab_ref[4 * blk + i, piece, q] for piece in range(PIECES) for q in range(QP)], axis=1
                )
                for i in range(4)
            ],
            axis=0,
        )
        y = jnp.dot(pick_ref[blk], x, preferred_element_type=F32).astype(BF16)
        rows_ref[:, pl.ds(pl.multiple_of(32 * blk, 32), 32), :] = y.reshape(8, 32, PIECES * KP)
        return carry

    def group(g, carry):
        for piece in range(PIECES):
            copy_ints(g, piece).wait()
        sum_ref[g] = sum(
            jnp.dot(
                rows_ref[g, :, KP * piece : KP * piece + KP],
                ints_ref[g, KP * piece : KP * piece + KP],
                preferred_element_type=F32,
            )
            for piece in range(PIECES)
        )
        return carry

    def unsort(blk, carry):
        x = sum_ref[:, pl.ds(pl.multiple_of(32 * blk, 32), 32), :].reshape(256, SA * RUN)
        hi, lo = two_terms(x)
        y = jnp.dot(drop_ref[blk], hi, preferred_element_type=F32)
        y = y + jnp.dot(drop_ref[blk], lo, preferred_element_type=F32)
        for i in range(4):
            got = y[32 * i : 32 * i + 32, :] + cycle_ref[4 * blk + i]

            @pl.when(core == i % 2)
            def _():
                keep_ref[2 * blk + i // 2] = got

            @pl.when(core != i % 2)
            def _():
                send_ref[2 * blk + i // 2] = got

        return carry

    copy_small(0).start()
    lax.fori_loop(0, OI, start, 0)
    for g in range(8):
        for piece in range(PIECES):
            copy_ints(g, piece).start()
    for n in (1, 2):
        copy_small(n).start()
    copy_small(0).wait()
    lax.fori_loop(0, 8, sort, 0)
    lax.fori_loop(0, 8, group, 0)
    for n in (1, 2):
        copy_small(n).wait()
    lax.fori_loop(0, 8, unsort, 0)


def ladder(where, core, arrived, pick, early, late, drop, cyc):
    smem = pl.BlockSpec(memory_space=pltpu.SMEM)
    vmem = pl.BlockSpec(memory_space=pltpu.VMEM)
    hbm = pl.BlockSpec(memory_space=pltpu.HBM)
    return pl.pallas_call(
        ladder_kernel,
        in_specs=[smem] * 2 + [hbm] * 13,
        out_specs=[vmem] * 2,
        out_shape=[jax.ShapeDtypeStruct((16, OJ, 512), F32)] * 2,
        scratch_shapes=[
            pltpu.VMEM((8, 256, PIECES * KP), BF16),
            pltpu.VMEM((OI, PIECES, QP, OJ, 128), BF16),
            pltpu.VMEM((8, PIECES * KP, 512), BF16),
            pltpu.VMEM((8, 256, 512), F32),
            pltpu.VMEM((8, 256, 128), BF16),
            pltpu.VMEM((8, 128, 256), BF16),
            pltpu.VMEM((OI, OJ, 512), F32),
            pltpu.SemaphoreType.DMA((OI, PIECES)),
            pltpu.SemaphoreType.DMA((PIECES, 8)),
            pltpu.SemaphoreType.DMA((3,)),
        ],
        compiler_params=pltpu.CompilerParams(vmem_limit_bytes=VMEM),
        cost_estimate=cost(5_400_000_000, 30 * 2**20),
        name="ladder",
    )(where, core, *[in_hbm(x) for x in (*arrived, early, late, pick, drop, cyc)])


def cycle_kernel(ovov_ref, amp_ref, want_ref, sym_ref, out_ref, mid_ref, turn_ref):
    acc = None
    for k in range(4):
        part = lax.dot_general(
            ovov_ref[:, NV * k : NV * k + NV],
            amp_ref[k].reshape(512, NV),
            (((1,), (1,)), ((), ())),
            preferred_element_type=F32,
        )
        acc = part if acc is None else acc + part
    low = lax.broadcasted_iota(jnp.int32, (OI, 128), 1) < 64
    for t in range(4):
        mid_ref[t] = acc[:, 128 * t : 128 * t + 128]
    for t in range(4):
        keep = [
            jnp.broadcast_to(want_ref[2 * t + e], (OI, 128)) for e in range(2)
        ]
        for m in range(4):
            x0 = mid_ref[t, pl.ds(2 * m, OI, stride=SA), :]
            x1 = mid_ref[t, pl.ds(2 * m + 1, OI, stride=SA), :]
            sym = sym_ref[0:1, 128 * m : 128 * m + 128]
            y0 = jnp.where(low, x0, pltpu.roll(x1, 64, 1))
            y1 = jnp.where(low, pltpu.roll(x0, 64, 1), x1)
            turn_ref[m, pl.ds(2 * t, OI, stride=8), :] = jnp.where(keep[0] == sym, y0, 0.0)
            turn_ref[m, pl.ds(2 * t + 1, OI, stride=8), :] = jnp.where(keep[1] == sym, y1, 0.0)
    for m in range(4):
        out_ref[:, :, 128 * m : 128 * m + 128] = turn_ref[m].reshape(OI, 8, 128)


def cycle_term(ovov, amp_t, want, sym):
    return pl.pallas_call(
        cycle_kernel,
        grid=(4,),
        in_specs=[
            pl.BlockSpec((OI * SA, 4 * NV), lambda s: (0, 0)),
            pl.BlockSpec((4, 8, RUN, NV), lambda s: (0, s, 0, 0)),
            pl.BlockSpec((8, OI, 1), lambda s: (s, 0, 0)),
            pl.BlockSpec((8, 512), lambda s: (0, 0)),
        ],
        out_specs=pl.BlockSpec((OI, 8, 512), lambda s: (0, s, 0)),
        out_shape=jax.ShapeDtypeStruct((OI, OJ, 512), F32),
        scratch_shapes=[pltpu.VMEM((4, OI * SA, 128), F32), pltpu.VMEM((4, OI * 8, 128), F32)],
        compiler_params=params(),
        cost_estimate=cost(2_100_000_000, 11 * 2**20),
        name="cycle_term",
    )(in_hbm(ovov), in_hbm(amp_t), want, sym)


def by_run_kernel(ltab_ref, x_ref, spread_ref, out_ref):
    hi, lo = two_terms(jnp.sum(x_ref[...], axis=0))
    y = jnp.dot(spread_ref[...], hi, preferred_element_type=F32)
    y = y + jnp.dot(spread_ref[...], lo, preferred_element_type=F32)
    for a in range(SA):
        for t in range(8):
            out_ref[ltab_ref[a, t], :, 64 * a : 64 * a + 64] = y[8 * t : 8 * t + 8, 64 * a : 64 * a + 64]


def by_run(ltab, x, spread):
    return pl.pallas_call(
        by_run_kernel,
        grid_spec=pltpu.PrefetchScalarGridSpec(
            num_scalar_prefetch=1,
            grid=(1,),
            in_specs=[
                pl.BlockSpec((ROWS, OJ, 512), lambda s, *_: (0, 0, 0)),
                pl.BlockSpec((64, OJ), lambda s, *_: (0, 0)),
            ],
            out_specs=pl.BlockSpec((8, 8, 512), lambda s, *_: (0, 0, 0)),
        ),
        out_shape=jax.ShapeDtypeStruct((8, 8, 512), F32),
        compiler_params=params(),
        name="by_run",
    )(ltab, x, spread)


def finish_kernel(slot_ref, irr_ref, energy_ref, x_ref, va_ref, vb_ref, sa_ref, sb_ref, out_ref, tile_ref):
    for h in range(2):
        v = x_ref[h]
        for y in range(1, 4):
            v = v + x_ref[2 * y + h]
        for a in range(SA):
            tile_ref[h, :, a, :] = v[:, 64 * a : 64 * a + 64]
    sym_ab = jnp.bitwise_xor(sa_ref[...], sb_ref[...])
    for h in range(2):
        for j in range(OJ):
            got = tile_ref[h, slot_ref[j]]
            den = energy_ref[h, j] - va_ref[...] - vb_ref[...]
            ok = jnp.bitwise_xor(sym_ab, irr_ref[h, j]) == 0
            out_ref[h, j] = jnp.where(ok, got / den, jnp.zeros_like(got))


def finish(slot, irr, energy, x, va, vb, sa, sb):
    full = lambda *dims: pl.BlockSpec(dims, lambda s, *_: (0,) * len(dims))
    return pl.pallas_call(
        finish_kernel,
        grid_spec=pltpu.PrefetchScalarGridSpec(
            num_scalar_prefetch=3,
            grid=(1,),
            in_specs=[full(8, 8, 512), full(8, 64), full(8, 64), full(8, 64), full(8, 64)],
            out_specs=full(2, OJ, SA, RUN),
            scratch_shapes=[pltpu.VMEM((2, 8, SA, RUN), F32)],
        ),
        out_shape=pltpu.HBM((2, OJ, SA, RUN), F32),
        compiler_params=params(),
        name="finish",
    )(slot, irr, energy, x, va, vb, sa, sb)


def body(
    slots,
    count,
    amplitudes,
    vvvv_ints,
    ovov_ints,
    occ_energy,
    vir_energy,
    occ_irrep,
    vir_irrep,
    i_orbitals,
    j_orbitals,
    a_orbitals,
):
    row = lax.axis_index("row")
    col = lax.axis_index("col")
    core = lax.rem(col, 2)
    labels = jnp.arange(8, dtype=jnp.int32)
    amp_t = amplitudes.transpose(0, 1, 3, 2)

    x_pos, z_pos = row // 4, row % 4
    lane = jnp.arange(4, dtype=jnp.int32)
    is_i = i_orbitals[:, None] == jnp.arange(NO)
    chosen = is_i.any(axis=0).reshape(4, 4, 4)
    if slots == 4:
        slot_of = jnp.broadcast_to(lane, (4, 4, 4))
        ktab = lane
    else:
        slot_of = jnp.sum(chosen[:, :, None, :] & (lane[:, None] > lane), axis=-1).astype(jnp.int32)
        own = lambda x: lax.dynamic_index_in_dim(x.reshape(ROWS, 4), row, keepdims=False)
        ktab = jnp.sum(jnp.where(own(chosen) & (own(slot_of) == lane[:, None]), lane, 0), axis=-1)
    ptab = jnp.concatenate([ktab, jnp.stack([x_pos, z_pos])]).astype(jnp.int32)
    packed = pack(amp_t, 1, slots, ptab)
    second = {n: move(packed[n], n, False) for n in (1, 3)}
    sent = [pack(amp_t, 0, slots, *after([ptab], packed[0])), packed]
    first = {n: move(sent[0][n], n, True) for n in (1, 3, 2)}

    line_before = jnp.arange(16)[:, None] > jnp.arange(16)
    others = jnp.arange(16, dtype=jnp.int32) // 4
    tabs, where = [], []
    for piece in range(2):
        mine, other = (x_pos, z_pos) if piece else (z_pos, x_pos)
        by_line = lambda x: (x if piece else x.transpose(1, 0, 2)).reshape(4, 16)
        line = by_line(chosen)
        rank = jnp.sum(line[:, None, :] & line_before, axis=-1).astype(jnp.int32)
        here, here_rank, here_slot = [
            lax.dynamic_index_in_dim(x, mine, keepdims=False) for x in (line, rank, by_line(slot_of))
        ]
        nth = here & (here_rank == jnp.arange(count)[:, None])
        nth_other = jnp.sum(jnp.where(nth, others, 0), axis=-1)
        nth_slot = jnp.sum(jnp.where(nth, here_slot, 0), axis=-1)
        tabs.append(jnp.stack([(other - nth_other) & 3, nth_slot, jnp.full_like(nth_slot, mine)]).astype(jnp.int32))
        rank = rank.reshape(4, 4, 4)
        rank = (rank if piece else rank.transpose(1, 0, 2)).reshape(NO)
        away = (mine - (i_orbitals // (16 if piece else 4)) % 4) & 3
        where.append(jnp.stack([away, jnp.sum(jnp.where(is_i, rank, 0), axis=-1)]).astype(jnp.int32))

    sym_i = jnp.take(occ_irrep, i_orbitals)
    sym_j = jnp.take(occ_irrep, j_orbitals)
    sym_a = jnp.take(vir_irrep, a_orbitals)
    run_label = vir_irrep.reshape(8, RUN)[:, 0]
    slot = j_orbitals % 8
    gtab = jnp.bitwise_xor(sym_a[:, None], run_label[None, :])
    g_ij = jnp.bitwise_xor(sym_i[:, None], sym_j[None, :])
    hit = (g_ij[:, :, None, None] == labels[:, None]) & (slot[:, None, None] == labels)
    hit = hit.reshape(8, 4, OJ, 8, 8)
    same = (jnp.arange(4)[:, None] == jnp.arange(4)).reshape(1, 4, 1, 1, 4, 1)
    drop = (hit[:, :, :, :, None, :] & same).reshape(8, 128, 256).astype(BF16)
    pick = drop.transpose(0, 2, 1)
    mine_label = lax.dynamic_index_in_dim(run_label, col, keepdims=False)
    want = jnp.bitwise_xor(g_ij.T, mine_label)[:, :, None]
    sym_lanes = jnp.broadcast_to(jnp.repeat(sym_a, RUN)[None, :], (8, SA * RUN))

    mine_i = lax.dynamic_slice_in_dim(i_orbitals, 2 * row, 2)
    sym_mine = jnp.take(occ_irrep, mine_i)
    label_at = jnp.bitwise_xor(
        jnp.bitwise_xor(lax.dynamic_index_in_dim(sym_mine, core, keepdims=False), sym_a)[:, None],
        labels[None, :],
    )
    ltab = jnp.sum(jnp.where(label_at[..., None] == run_label, labels, 0), axis=-1).astype(jnp.int32)
    spread = (
        (sym_j[None, None, :] == labels[:, None, None]) & (slot[None, None, :] == labels[None, :, None])
    ).reshape(64, OJ).astype(BF16)
    energy = jnp.take(occ_energy, mine_i)[:, None] + jnp.take(occ_energy, j_orbitals)[None, :]
    irr = jnp.bitwise_xor(sym_mine[:, None], sym_j[None, :])
    wide = lambda x: jnp.broadcast_to(x, (SA, RUN))
    va = wide(jnp.take(vir_energy, a_orbitals)[:, None])
    vb = wide(lax.dynamic_slice_in_dim(vir_energy, col * RUN, RUN)[None, :])
    sa = wide(sym_a[:, None])
    sb = wide(lax.dynamic_slice_in_dim(vir_irrep, col * RUN, RUN)[None, :])
    tail = (ltab, spread, slot, irr, energy, va, vb, sa, sb)

    ints = vvvv_ints.reshape(32, 512, NV)
    (held,) = after([sent[1][2]], second[1], second[3])
    second[2] = move(held, 2, False)
    (want,) = after([want], second[1], second[3])
    cyc = cycle_term(ovov_ints.reshape(OI * SA, 4 * NV), amp_t, want, sym_lanes)
    (gate,) = after([gtab], cyc)
    early = arrange_ints(0, 1, gate, ints, pltpu.HBM)
    (tab1,) = after([tabs[1]], early, pick, *tail)
    lines1 = [sent[1][0], second[1], second[2], second[3]]
    sides1 = regroup(tab1, lines1, 1, 3)
    (tab0,) = after([tabs[0]], sides1)
    lines0 = [sent[0][0], first[1], first[2], first[3]]
    sides0 = regroup(tab0, lines0, 1, 3, 2)
    arrived0 = {n: move(x, n, False) for n, x in zip((1, 3, 2), sides0)}
    sides1 = after(sides1, first[1], first[2], first[3])
    arrived1 = {n: move(x, n, True) for n, x in zip((1, 3), sides1)}
    rest1, rest0 = after([tab1, tab0], sides0)
    across1, arrived1[0] = regroup(rest1, lines1, 2, 0)
    (arrived0[0],) = regroup(rest0, lines0, 0)
    (across1,) = after([across1], arrived1[1], arrived1[3])
    (gate,) = after([gtab], across1, arrived0[0], *tail)
    arrived1[2] = move(across1, 2, True)
    late = arrange_ints(1, 1, gate, ints, pltpu.HBM)
    keep, give = ladder(
        jnp.concatenate(where),
        core.reshape(1),
        [arrived0[n] for n in range(4)] + [arrived1[n] for n in range(4)],
        pick, early, late, drop, cyc,
    )

    got = lax.ppermute(give, "col", [(q, q ^ 1) for q in range(COLS)])
    both = lax.all_to_all(keep + got, "row", split_axis=0, concat_axis=0, tiled=True)
    parts = lax.all_to_all(by_run(ltab, both, spread), "col", split_axis=0, concat_axis=0, tiled=True)
    return finish(slot, irr, energy, parts, va, vb, sa, sb)


def shards(*args):
    spots = jnp.stack([args[7] // 16, args[7] // 4 % 4])
    on_line = jnp.max(jnp.sum(spots[:, None, :] == jnp.arange(4)[:, None], axis=-1))
    return lax.cond(
        on_line > 12, functools.partial(body, 4, 16), functools.partial(body, 4, 12), *args
    )


def solution(mesh):
    return jax.shard_map(
        shards,
        mesh=mesh,
        in_specs=(
            P("row", None, None, "col"),
            P("row", "col", None, None),
            P(None, None, "row", None),
            P(),
            P(),
            P(),
            P(),
            P(),
            P(),
            P(),
        ),
        out_specs=P("row", None, None, "col"),
        check_vma=False,
    )
```
